256 devices in a mesh: row: 32 (over y, x, core), col: 8 (over z).
Axes of the slice: x: 4, y: 4, z: 8, core: 2. Of those that a mesh axis runs over, the one named last changes fastest.
Arguments:
- check_field: bfloat16 [2, 152, 131072], P(None, None, ('row', 'col')), may hold values from -6 to 6
- to_equiv: bfloat16 [2, 152, 152], replicated, may hold values from -0.3125 to 0.3125
- upward_ops: bfloat16 [4, 8, 2, 152, 152], replicated, may hold values from -0.125 to 0.125
- downward_ops: bfloat16 [4, 8, 2, 152, 152], replicated, may hold values from -0.3125 to 0.3125
- transfer_ops: bfloat16 [4, 16, 2, 152, 152], replicated, may hold values from -0.078125 to 0.078125
- list_fine: int32 [131072, 16], P(('row', 'col')), may hold values from 0 to 131071, as said below
- list_mid: int32 [16384, 16], P(('row', 'col')), may hold values from 0 to 16383, as said below
- list_low: int32 [2048, 16], P(('row', 'col')), may hold values from 0 to 2047, as said below
- list_top: int32 [32, 16], replicated, may hold values from 0 to 31, as said below
Outputs:
- far_field: float32 [2, 152, 131072], P(None, None, ('row', 'col'))
The draws below stay inside these ranges and needn't reach their ends.
Inputs may be any that keep to these rules, and one draw needn't show every extreme that they name: `list_fine`: each source lies within 256 of its target box index. `list_mid`: each source lies within 32 of its target box index. `list_low`: each source lies within 4 of its target box index. `list_top`: no box lists itself.
All inputs are finite; a program needn't handle non-finite values.
Results may differ from the reference program's by a relative error of at most 0.014.
Values may be sent and summed in bfloat16 or wider, within the bound.
No kernel may reach another device: no remote copies, remote signals or barrier semaphores. Data moves between devices by JAX's collectives and lax.ppermute only.
A program may use at most 128 MiB of HBM per device.

```python
import jax
import jax.numpy as jnp
from jax import lax

P_SIZE = 152
K = 16
BOX_DEV = 512
BOXES7 = 131072
BOXES6 = 16384
BOXES5 = 2048
BOXES3 = 32
N_ROW = 32
N_COL = 8


def spread_list(key, box_count, reach):
    targets = jnp.arange(box_count, dtype=jnp.int32)[:, None]
    slot_ids = jnp.arange(K, dtype=jnp.int32)[None, :]
    distance = jax.random.randint(key, (box_count, K), 1, reach + 1, dtype=jnp.int32)
    direction = jax.random.randint(jax.random.fold_in(key, 1), (box_count, K), 0, 2, dtype=jnp.int32) * 2 - 1
    distance = jnp.where(slot_ids < 2, reach, distance)
    direction = jnp.where(slot_ids == 0, 1, jnp.where(slot_ids == 1, -1, direction))
    sources = targets + direction * distance
    sources = jnp.where(sources > box_count - 1, targets - distance, sources)
    sources = jnp.where(sources < 0, targets + distance, sources)
    return sources.astype(jnp.int32)


def draw_list_fine(key, part):
    key = jax.random.fold_in(key, 11)
    return spread_list(key, BOXES7, BOX_DEV // 2)


def draw_list_mid(key, part):
    key = jax.random.fold_in(key, 12)
    return spread_list(key, BOXES6, BOX_DEV // 16)


def draw_list_low(key, part):
    key = jax.random.fold_in(key, 13)
    return spread_list(key, BOXES5, BOX_DEV // 128)


def draw_list_top(key, part):
    key = jax.random.fold_in(key, 14)
    targets = jnp.arange(BOXES3, dtype=jnp.int32)[:, None]
    slot_ids = jnp.arange(K, dtype=jnp.int32)[None, :]
    stride = jax.random.randint(key, (BOXES3, K), 1, BOXES3, dtype=jnp.int32)
    stride = jnp.where(slot_ids == 0, 1, stride)
    return jnp.remainder(targets + stride, BOXES3).astype(jnp.int32)


def shard_levels(stream_key, shape, shards, smallest, high):
    def one(dim, parts):
        heights = jax.random.uniform(jax.random.fold_in(jax.random.fold_in(stream_key, 6), dim), (parts,), jnp.float32, smallest / len(shards), high / len(shards))
        return jnp.repeat(jnp.exp(heights), shape[dim] // parts).reshape((-1,) + (1,) * (len(shape) - dim - 1))

    level = one(*shards[0])
    for cut in shards[1:]:
        level = level * one(*cut)
    return level


def gaussian(own_key, extent, scale, limit, pieces=(), kind=jnp.bfloat16):
    result = jax.random.normal(own_key, extent, jnp.float32) * scale
    if len(pieces) > 0:
        result = shard_levels(own_key, extent, pieces, -0.22, 0.18) * result
    return jnp.clip(result, min=-limit, max=limit).astype(kind)


def setup_inputs(seed: int = 0) -> dict:
    streams_of = jax.random.split(jax.random.key(seed), 10)
    check_field = gaussian(streams_of[0], (2, P_SIZE, BOXES7), 1.0, 6.0, ((2, 256),))
    to_equiv = gaussian(streams_of[1], (2, P_SIZE, P_SIZE), (2 * P_SIZE) ** -0.5, 0.3125)
    upward_ops = gaussian(streams_of[2], (4, 8, 2, P_SIZE, P_SIZE), (16 * P_SIZE) ** -0.5, 0.125)
    downward_ops = gaussian(streams_of[3], (4, 8, 2, P_SIZE, P_SIZE), (2 * P_SIZE) ** -0.5, 0.3125)
    transfer_ops = gaussian(streams_of[4], (4, K, 2, P_SIZE, P_SIZE), (2 * P_SIZE * K) ** -0.5, 0.078125)
    list_fine = draw_list_fine(jax.random.fold_in(streams_of[9], 71), 0)
    list_mid = draw_list_mid(jax.random.fold_in(streams_of[9], 71), 0)
    list_low = draw_list_low(jax.random.fold_in(streams_of[9], 71), 0)
    list_top = draw_list_top(jax.random.fold_in(streams_of[9], 71), 0)
    return {"check_field": check_field, "to_equiv": to_equiv, "upward_ops": upward_ops, "downward_ops": downward_ops, "transfer_ops": transfer_ops, "list_fine": list_fine, "list_mid": list_mid, "list_low": list_low, "list_top": list_top}


def realify(operators):
    real_part = operators[..., 0, :, :]
    imag_part = operators[..., 1, :, :]
    upper_rows = jnp.concatenate([real_part, -imag_part], axis=-1)
    lower_rows = jnp.concatenate([imag_part, real_part], axis=-1)
    return jnp.concatenate([upper_rows, lower_rows], axis=-2)


def lift_level(densities, operators):
    stack_width = densities.shape[0]
    parents = densities.shape[1] // 8
    grouped = densities.reshape(stack_width, parents, 8).astype(jnp.float32)
    return jnp.einsum('cij,jmc->im', operators.astype(jnp.float32), grouped).astype(jnp.bfloat16)


def spread(expansion, operators):
    stack_width, box_count = expansion.shape
    rounded = expansion.astype(jnp.bfloat16).astype(jnp.float32)
    children = jnp.einsum('cij,jm->imc', operators.astype(jnp.float32), rounded)
    return children.reshape(stack_width, box_count * operators.shape[0])


def translate_all(densities, operators, sources):
    stack_width, box_count = densities.shape

    def add_entry(entry_slot, running_sum):
        columns = jnp.take(densities, sources[:, entry_slot], axis=1)
        operator = lax.dynamic_index_in_dim(operators, entry_slot, 0, keepdims=False)
        return running_sum + jnp.dot(operator, columns, preferred_element_type=jnp.float32)

    return lax.fori_loop(0, sources.shape[1], add_entry, jnp.zeros((stack_width, box_count), jnp.float32))


def reference(check_field, to_equiv, upward_ops, downward_ops, transfer_ops, list_fine, list_mid, list_low, list_top):
    stack_width = 2 * P_SIZE
    dense_fine = jnp.dot(realify(to_equiv), check_field.reshape(stack_width, -1), preferred_element_type=jnp.float32).astype(jnp.bfloat16)
    dense_mid = lift_level(dense_fine, realify(upward_ops[0]))
    dense_low = lift_level(dense_mid, realify(upward_ops[1]))
    dense_four = lift_level(dense_low, realify(upward_ops[2]))
    grouped = dense_four.reshape(stack_width, N_ROW, N_COL).astype(jnp.float32)
    dense_top = jnp.einsum('cij,jrc->ir', realify(upward_ops[3])[:N_COL].astype(jnp.float32), grouped).astype(jnp.bfloat16)
    local_top = translate_all(dense_top, realify(transfer_ops[3]), list_top)
    top_rounded = local_top.astype(jnp.bfloat16).astype(jnp.float32)
    local_four = jnp.einsum('cij,jr->irc', realify(downward_ops[3])[:N_COL].astype(jnp.float32), top_rounded)
    local_four = local_four.reshape(stack_width, N_ROW * N_COL)
    local_low = spread(local_four, realify(downward_ops[2])) + translate_all(dense_low, realify(transfer_ops[2]), list_low)
    local_mid = spread(local_low, realify(downward_ops[1])) + translate_all(dense_mid, realify(transfer_ops[1]), list_mid)
    local_fine = spread(local_mid, realify(downward_ops[0])) + translate_all(dense_fine, realify(transfer_ops[0]), list_fine)
    return local_fine.reshape(2, P_SIZE, -1)
```

```python
import functools

import jax
import jax.numpy as jnp
from jax import lax
from jax.experimental import pallas as pl
from jax.experimental.pallas import tpu as pltpu
from jax.sharding import PartitionSpec as P

SIZE = 152
HALF = 64
FINE = 512
REACH = 256
ENTRIES = 16
OCTANTS = 8
BF16 = jnp.bfloat16
F32 = jnp.float32


def mm(a, b):
    return jnp.dot(a, b, preferred_element_type=F32)


def iota(shape, dim):
    return lax.broadcasted_iota(jnp.int32, shape, dim)


def combine(by_real, by_imag):
    turned = pltpu.roll(by_imag, HALF, 1)
    return by_real + jnp.where(iota(turned.shape, 1) < HALF, -turned, turned)


def child_columns(level):
    del level
    row = iota((128, 1024), 0)
    col = iota((128, 1024), 1)
    octant, lane = col >> 7, col & 127
    box = (lane & 63) * 8 + octant
    wanted = jnp.where(box < HALF, (lane & HALF) + box, -1)
    return (row == wanted).astype(BF16)


def parent_columns():
    row = iota((128, 1024), 0)
    col = iota((128, 1024), 1)
    octant, lane = col >> 7, col & 127
    box = lane & 63
    wanted = jnp.where((box & 7) == octant, (lane & HALF) + (box >> 3), -1)
    return (row == wanted).astype(BF16)


def up_kernel(col_ref, check, to_equiv, ops_hbm, to_left, to_right, top, ops, own_op, sems):
    copies = [
        pltpu.make_async_copy(ops_hbm.at[level], ops.at[level], sems.at[level])
        for level in range(3)
    ]
    copies.append(pltpu.make_async_copy(ops_hbm.at[3, col_ref[0]], own_op, sems.at[3]))
    for copy in copies:
        copy.start()
    field = jnp.concatenate([check[0], check[1]], axis=1)
    by_real = mm(to_equiv[0], field)
    by_imag = mm(to_equiv[1], field)
    real = (by_real[:, :FINE] - by_imag[:, FINE:]).astype(BF16)
    imag = (by_real[:, FINE:] + by_imag[:, :FINE]).astype(BF16)
    to_left[:, :REACH] = jnp.concatenate([real[:, :REACH], imag[:, :REACH]], axis=0)
    to_right[:, :REACH] = jnp.concatenate([real[:, REACH:], imag[:, REACH:]], axis=0)

    row = iota((FINE, 1024), 0)
    col = iota((FINE, 1024), 1)
    octant, lane = col >> 7, col & 127
    box = (lane & 63) * 8 + octant
    of_real = (row == jnp.where(lane < HALF, box, -1)).astype(BF16)
    of_imag = (row == jnp.where(lane >= HALF, box, -1)).astype(BF16)
    children = (mm(real, of_real) + mm(imag, of_imag)).astype(BF16)
    pick = child_columns(0)
    packed = []
    for level in range(3):
        copies[level].wait()
        by_real = jnp.zeros((SIZE, 128), F32)
        by_imag = jnp.zeros((SIZE, 128), F32)
        for c in range(OCTANTS):
            one = children[:, 128 * c : 128 * (c + 1)]
            by_real += mm(ops[level, c, 0], one)
            by_imag += mm(ops[level, c, 1], one)
        dense = combine(by_real, by_imag).astype(BF16)
        packed.append(dense)
        if level < 2:
            children = mm(dense, pick).astype(BF16)
    both = jnp.concatenate([packed[0].astype(F32), packed[1].astype(F32)], axis=0).astype(BF16)
    to_left[:, REACH:] = both
    to_right[:, REACH:] = both
    copies[3].wait()
    part = combine(mm(own_op[0], packed[2]), mm(own_op[1], packed[2]))
    flat = jnp.transpose(jnp.concatenate([part, jnp.zeros((104, 128), F32)], axis=0))
    top[0:1, :] = flat[0:1, :]
    top[1:2, :] = flat[HALF : HALF + 1, :]


def translate_packed(around, codes, targets, ops_pair):
    by_real = jnp.zeros((SIZE, 128), F32)
    by_imag = jnp.zeros((SIZE, 128), F32)
    for k in range(ENTRIES):
        select = (codes == targets[k : k + 1, :]).astype(BF16)
        picked = mm(around, select).astype(BF16)
        by_real += mm(ops_pair[k, 0], picked)
        by_imag += mm(ops_pair[k, 1], picked)
    return combine(by_real, by_imag)


def near_kernel(
    start_ref, from_left, from_right, to_left, to_right, fine_t, mid_t, low_t, ops_hbm,
    fine_out, mid_out, low_out, around, ops, sems,
):
    copies = [
        pltpu.make_async_copy(ops_hbm.at[level], ops.at[level], sems.at[level])
        for level in range(3)
    ]
    for level in (2, 1, 0):
        copies[level].start()
    position = start_ref[0]
    around[:, 0:REACH] = from_left[:, :REACH]
    around[:, REACH : 2 * REACH] = to_left[:, :REACH]
    around[:, 2 * REACH : 3 * REACH] = to_right[:, :REACH]
    around[:, 3 * REACH :] = from_right[:, :REACH]

    lows = [ref[SIZE:, REACH:].astype(F32) for ref in (to_left, from_left, from_right)]
    low_all = (lows[0] + pltpu.roll(lows[1], 8, 1) + pltpu.roll(lows[2], 16, 1)).astype(BF16)
    row = iota((128, 128), 0)
    lane = row & 63
    place = jnp.where(lane < 8, lane, jnp.where(lane < 16, lane - 16, lane - 8))
    codes = jnp.where(lane < 24, (row >> 6) * 1024 + place, -(1 << 20))
    low_index = low_t[...] - position * 8
    pad = jnp.full((ENTRIES, HALF - 8), -(1 << 19), jnp.int32)
    targets = jnp.concatenate([low_index, pad, low_index + 1024, pad], axis=1)
    copies[2].wait()
    low_out[...] = translate_packed(low_all, codes, targets, ops.at[2])

    mid_all = jnp.concatenate(
        [from_left[:SIZE, REACH:], to_left[:SIZE, REACH:], from_right[:SIZE, REACH:]], axis=1
    )
    row = iota((384, 128), 0)
    codes = ((row >> 6) & 1) * 1024 + (row & 63) + ((row >> 7) - 1) * HALF
    mid_index = mid_t[...] - position * HALF
    targets = jnp.concatenate([mid_index, mid_index + 1024], axis=1)
    copies[1].wait()
    mid_out[...] = translate_packed(mid_all, codes, targets, ops.at[1])

    copies[0].wait()
    row = iota((3 * REACH, REACH), 0)
    for half in range(2):
        start = half * REACH
        window = around[:, start : start + 3 * REACH]
        index = fine_t[:, start : start + REACH] - (position * FINE - REACH + start)
        by_real = jnp.zeros((SIZE, FINE), F32)
        by_imag = jnp.zeros((SIZE, FINE), F32)
        for k in range(ENTRIES):
            select = (row == index[k : k + 1, :]).astype(BF16)
            picked = mm(window, select)
            picked = jnp.concatenate([picked[:SIZE], picked[SIZE:]], axis=1).astype(BF16)
            by_real += mm(ops[0, k, 0], picked)
            by_imag += mm(ops[0, k, 1], picked)
        fine_out[0, :, start : start + REACH] = by_real[:, :REACH] - by_imag[:, REACH:]
        fine_out[1, :, start : start + REACH] = by_real[:, REACH:] + by_imag[:, :REACH]


def down_kernel(
    col_ref, tops, own_list, fine_near, mid_near, low_near, transfer_hbm, down_hbm, out,
    transfer, down, own_op, sems,
):
    copies = [
        pltpu.make_async_copy(down_hbm.at[level], down.at[level], sems.at[level])
        for level in range(3)
    ]
    copies.append(pltpu.make_async_copy(down_hbm.at[3, col_ref[0]], own_op, sems.at[3]))
    copies.append(pltpu.make_async_copy(transfer_hbm.at[3], transfer, sems.at[4]))
    for level in (4, 3, 2, 1, 0):
        copies[level].start()

    gap = jnp.zeros((HALF - tops.shape[1], 256), F32)
    rows = jnp.concatenate([tops[0], gap, tops[1], gap], axis=0)
    dense = jnp.transpose(rows)[:SIZE].astype(BF16)
    row = iota((128, 128), 0)
    lane = iota((128, 128), 1)
    listed = own_list[...]
    pad = jnp.full((1, HALF - ENTRIES), -(1 << 19), jnp.int32)
    wanted = jnp.concatenate([listed, pad, listed + HALF, pad], axis=1)
    picked = mm(dense, (row == wanted).astype(BF16))
    lane = iota((SIZE, 128), 1)
    copies[4].wait()
    by_real = jnp.zeros((SIZE, 128), F32)
    by_imag = jnp.zeros((SIZE, 128), F32)
    for k in range(ENTRIES):
        one = jnp.where((lane & 63) == k, picked, 0.0).astype(BF16)
        by_real += mm(transfer[k, 0], one)
        by_imag += mm(transfer[k, 1], one)
    local = combine(by_real, by_imag)
    for shift in (8, 4, 2, 1):
        local = local + pltpu.roll(local, 128 - shift, 1)
    local = jnp.where((lane & 63) == 0, local, 0.0).astype(BF16)
    copies[3].wait()
    local = combine(mm(own_op[0], local), mm(own_op[1], local)).astype(BF16)
    place = parent_columns()
    for level, near in ((2, low_near), (1, mid_near)):
        parents = mm(local, place).astype(BF16)
        copies[level].wait()
        by_real = jnp.zeros((SIZE, 128), F32)
        by_imag = jnp.zeros((SIZE, 128), F32)
        for c in range(OCTANTS):
            one = parents[:, 128 * c : 128 * (c + 1)]
            by_real += mm(down[level, c, 0], one)
            by_imag += mm(down[level, c, 1], one)
        local = (combine(by_real, by_imag) + near[...]).astype(BF16)
    copies[0].wait()
    row = iota((128, 1024), 0)
    col = iota((128, 1024), 1)
    by_real = jnp.zeros((SIZE, 1024), F32)
    by_imag = jnp.zeros((SIZE, 1024), F32)
    child = col & (FINE - 1)
    source = (col >> 9) * HALF + (child >> 3)
    for c in range(OCTANTS):
        spread = (row == jnp.where((child & 7) == c, source, -1)).astype(BF16)
        parents = mm(local, spread).astype(BF16)
        by_real += mm(down[0, c, 0], parents)
        by_imag += mm(down[0, c, 1], parents)
    out[0] = fine_near[0] + (by_real[:, :FINE] - by_imag[:, FINE:])
    out[1] = fine_near[1] + (by_real[:, FINE:] + by_imag[:, :FINE])


def shape(dims, dtype):
    return jax.ShapeDtypeStruct(dims, dtype)


VMEM = pl.BlockSpec(memory_space=pltpu.VMEM)
SMEM = pl.BlockSpec(memory_space=pltpu.SMEM)
ANY = pl.BlockSpec(memory_space=pl.ANY)
INTERPRET = False


def call(kernel, ins, outs, scratch, flops, limit=40):
    return pl.pallas_call(
        kernel,
        in_specs=ins,
        out_specs=[VMEM] * len(outs),
        out_shape=outs,
        scratch_shapes=scratch,
        compiler_params=pltpu.CompilerParams(vmem_limit_bytes=limit << 20),
        cost_estimate=pl.CostEstimate(flops=flops, bytes_accessed=8 << 20, transcendentals=0),
        interpret=INTERPRET,
    )


def body(
    check_field, to_equiv, upward_ops, downward_ops, transfer_ops, list_fine, list_mid, list_low, list_top
):
    axes = ("row", "col")
    rows, cols = lax.axis_size("row"), lax.axis_size("col")
    count = rows * cols
    position = lax.axis_index(axes).astype(jnp.int32).reshape(1)
    own_col = lax.axis_index("col").astype(jnp.int32).reshape(1)
    octant_ops = (2, SIZE, SIZE)
    to_left, to_right, top = call(
        up_kernel,
        [SMEM, VMEM, VMEM, ANY],
        [shape((2 * SIZE, 384), BF16), shape((2 * SIZE, 384), BF16), shape((2, 256), F32)],
        [
            pltpu.VMEM((3, OCTANTS) + octant_ops, BF16),
            pltpu.VMEM(octant_ops, BF16),
            pltpu.SemaphoreType.DMA((4,)),
        ],
        4 << 30,
    )(own_col, check_field, to_equiv, upward_ops)
    from_left = lax.ppermute(to_right, axes, [(i, (i + 1) % count) for i in range(count)])
    from_right = lax.ppermute(to_left, axes, [(i, (i - 1) % count) for i in range(count)])
    tops = gather_top(top)
    fine, mid, low = call(
        near_kernel,
        [SMEM] + [VMEM] * 7 + [ANY],
        [shape((2, SIZE, FINE), F32), shape((SIZE, 128), F32), shape((SIZE, 128), F32)],
        [
            pltpu.VMEM((2 * SIZE, 1024), BF16),
            pltpu.VMEM((3, ENTRIES) + octant_ops, BF16),
            pltpu.SemaphoreType.DMA((3,)),
        ],
        30 << 30,
    )(position, from_left, from_right, to_left, to_right, list_fine.T, list_mid.T, list_low.T, transfer_ops)
    own_list = lax.dynamic_slice_in_dim(list_top, lax.axis_index("row"), 1, 0)
    (far,) = call(
        down_kernel,
        [SMEM] + [VMEM] * 5 + [ANY, ANY],
        [shape((2, SIZE, FINE), F32)],
        [
            pltpu.VMEM((ENTRIES,) + octant_ops, BF16),
            pltpu.VMEM((3, OCTANTS) + octant_ops, BF16),
            pltpu.VMEM(octant_ops, BF16),
            pltpu.SemaphoreType.DMA((5,)),
        ],
        8 << 30,
    )(own_col, tops, own_list, fine, mid, low, transfer_ops, downward_ops)
    return far


def gather_top(top):
    total = lax.psum(top, "col").astype(BF16)
    return jnp.transpose(lax.all_gather(total, "row", axis=0), (1, 0, 2)).astype(F32)


def solution(mesh):
    split = P(None, None, ("row", "col"))
    lists = P(("row", "col"), None)
    return jax.shard_map(
        body,
        mesh=mesh,
        in_specs=(split, P(), P(), P(), P(), lists, lists, lists, P()),
        out_specs=split,
        check_vma=False,
    )
```

```python
import functools

import jax
import jax.numpy as jnp
from jax import lax
from jax.experimental import pallas as pl
from jax.experimental.pallas import tpu as pltpu
from jax.sharding import PartitionSpec as P

SIZE = 152
HALF = 64
FINE = 512
REACH = 256
ENTRIES = 16
OCTANTS = 8
BF16 = jnp.bfloat16
F32 = jnp.float32


def mm(a, b):
    return jnp.dot(a, b, preferred_element_type=F32)


def iota(shape, dim):
    return lax.broadcasted_iota(jnp.int32, shape, dim)


def combine(by_real, by_imag):
    turned = pltpu.roll(by_imag, HALF, 1)
    return by_real + jnp.where(iota(turned.shape, 1) < HALF, -turned, turned)


def child_columns(level):
    del level
    row = iota((128, 1024), 0)
    col = iota((128, 1024), 1)
    octant, lane = col >> 7, col & 127
    box = (lane & 63) * 8 + octant
    wanted = jnp.where(box < HALF, (lane & HALF) + box, -1)
    return (row == wanted).astype(BF16)


def parent_columns():
    row = iota((128, 1024), 0)
    col = iota((128, 1024), 1)
    octant, lane = col >> 7, col & 127
    box = lane & 63
    wanted = jnp.where((box & 7) == octant, (lane & HALF) + (box >> 3), -1)
    return (row == wanted).astype(BF16)


def up_kernel(col_ref, check, to_equiv, ops_hbm, to_left, to_right, top, ops, own_op, sems):
    copies = [
        pltpu.make_async_copy(ops_hbm.at[level], ops.at[level], sems.at[level])
        for level in range(3)
    ]
    copies.append(pltpu.make_async_copy(ops_hbm.at[3, col_ref[0]], own_op, sems.at[3]))
    for copy in copies:
        copy.start()
    field = jnp.concatenate([check[0], check[1]], axis=1)
    by_real = mm(to_equiv[0], field)
    by_imag = mm(to_equiv[1], field)
    real = (by_real[:, :FINE] - by_imag[:, FINE:]).astype(BF16)
    imag = (by_real[:, FINE:] + by_imag[:, :FINE]).astype(BF16)
    to_left[:, :REACH] = jnp.concatenate([real[:, :REACH], imag[:, :REACH]], axis=0)
    to_right[:, :REACH] = jnp.concatenate([real[:, REACH:], imag[:, REACH:]], axis=0)

    row = iota((FINE, 1024), 0)
    col = iota((FINE, 1024), 1)
    octant, lane = col >> 7, col & 127
    box = (lane & 63) * 8 + octant
    of_real = (row == jnp.where(lane < HALF, box, -1)).astype(BF16)
    of_imag = (row == jnp.where(lane >= HALF, box, -1)).astype(BF16)
    children = (mm(real, of_real) + mm(imag, of_imag)).astype(BF16)
    pick = child_columns(0)
    packed = []
    for level in range(3):
        copies[level].wait()
        by_real = jnp.zeros((SIZE, 128), F32)
        by_imag = jnp.zeros((SIZE, 128), F32)
        for c in range(OCTANTS):
            one = children[:, 128 * c : 128 * (c + 1)]
            by_real += mm(ops[level, c, 0], one)
            by_imag += mm(ops[level, c, 1], one)
        dense = combine(by_real, by_imag).astype(BF16)
        packed.append(dense)
        if level < 2:
            children = mm(dense, pick).astype(BF16)
    both = jnp.concatenate([packed[0].astype(F32), packed[1].astype(F32)], axis=0).astype(BF16)
    to_left[:, REACH:] = both
    to_right[:, REACH:] = both
    copies[3].wait()
    part = combine(mm(own_op[0], packed[2]), mm(own_op[1], packed[2]))
    flat = jnp.transpose(jnp.concatenate([part, jnp.zeros((104, 128), F32)], axis=0))
    top[:, :256] = flat[0:1, :]
    top[:, 256:] = flat[HALF : HALF + 1, :]


def translate_packed(around, codes, targets, ops_pair):
    by_real = jnp.zeros((SIZE, 128), F32)
    by_imag = jnp.zeros((SIZE, 128), F32)
    for k in range(ENTRIES):
        select = (codes == targets[k : k + 1, :]).astype(BF16)
        picked = mm(around, select).astype(BF16)
        by_real += mm(ops_pair[k, 0], picked)
        by_imag += mm(ops_pair[k, 1], picked)
    return combine(by_real, by_imag)


def small_kernel(
    start_ref, ride, from_left, from_right, to_left, to_right, mid_t, low_t, ops_hbm,
    ride_out, mid_out, low_out, ops, sems,
):
    ride_out[...] = ride[...]
    copies = {
        level: pltpu.make_async_copy(ops_hbm.at[level], ops.at[level - 1], sems.at[level - 1])
        for level in (2, 1)
    }
    for copy in copies.values():
        copy.start()
    position = start_ref[0]
    lows = [ref[SIZE:, REACH:].astype(F32) for ref in (to_left, from_left, from_right)]
    low_all = (lows[0] + pltpu.roll(lows[1], 8, 1) + pltpu.roll(lows[2], 16, 1)).astype(BF16)
    row = iota((128, 128), 0)
    lane = row & 63
    place = jnp.where(lane < 8, lane, jnp.where(lane < 16, lane - 16, lane - 8))
    codes = jnp.where(lane < 24, (row >> 6) * 1024 + place, -(1 << 20))
    low_index = low_t[...] - position * 8
    pad = jnp.full((ENTRIES, HALF - 8), -(1 << 19), jnp.int32)
    targets = jnp.concatenate([low_index, pad, low_index + 1024, pad], axis=1)
    copies[2].wait()
    low_out[...] = translate_packed(low_all, codes, targets, ops.at[1])

    mid_all = jnp.concatenate(
        [from_left[:SIZE, REACH:], to_left[:SIZE, REACH:], from_right[:SIZE, REACH:]], axis=1
    )
    row = iota((384, 128), 0)
    codes = ((row >> 6) & 1) * 1024 + (row & 63) + ((row >> 7) - 1) * HALF
    mid_index = mid_t[...] - position * HALF
    targets = jnp.concatenate([mid_index, mid_index + 1024], axis=1)
    copies[1].wait()
    mid_out[...] = translate_packed(mid_all, codes, targets, ops.at[0])


def fine_kernel(
    half, start_ref, ride, before, first, second, fine_t, ops_hbm, ride_out, out, window, ops, sem
):
    ride_out[...] = ride[...]
    copy = pltpu.make_async_copy(ops_hbm.at[0], ops, sem)
    copy.start()
    window[:, :REACH] = before[:, :REACH]
    window[:, REACH : 2 * REACH] = first[:, :REACH]
    window[:, 2 * REACH :] = second[:, :REACH]
    index = fine_t[...] - (start_ref[0] * FINE + (half - 1) * REACH)
    row = iota((3 * REACH, REACH), 0)
    by_real = jnp.zeros((SIZE, FINE), F32)
    by_imag = jnp.zeros((SIZE, FINE), F32)
    copy.wait()
    for k in range(ENTRIES):
        select = (row == index[k : k + 1, :]).astype(BF16)
        picked = mm(window[...], select)
        picked = jnp.concatenate([picked[:SIZE], picked[SIZE:]], axis=1).astype(BF16)
        by_real += mm(ops[k, 0], picked)
        by_imag += mm(ops[k, 1], picked)
    out[0] = by_real[:, :REACH] - by_imag[:, REACH:]
    out[1] = by_real[:, REACH:] + by_imag[:, :REACH]


def down_kernel(
    col_ref, own_ref, tops, own_list, fine_near_a, fine_near_b, mid_near, low_near, transfer_hbm, down_hbm, out,
    transfer, down, own_op, sems,
):
    copies = [
        pltpu.make_async_copy(down_hbm.at[level], down.at[level], sems.at[level])
        for level in range(3)
    ]
    copies.append(pltpu.make_async_copy(down_hbm.at[3, col_ref[0]], own_op, sems.at[3]))
    copies.append(pltpu.make_async_copy(transfer_hbm.at[3], transfer, sems.at[4]))
    for level in (4, 3, 2, 1, 0):
        copies[level].start()

    gap = jnp.zeros((HALF - tops.shape[0], 256), F32)
    wide = tops[...].astype(F32)
    rows = jnp.concatenate([wide[:, :256], gap, wide[:, 256:], gap], axis=0)
    dense = jnp.transpose(rows)[:SIZE].astype(BF16)
    row = iota((128, 128), 0)
    lane = iota((128, 128), 1)
    listed = own_list[...] ^ own_ref[0]
    listed = listed ^ ((listed >> 1) & 0b01010)
    pad = jnp.full((1, HALF - ENTRIES), -(1 << 19), jnp.int32)
    wanted = jnp.concatenate([listed, pad, listed + HALF, pad], axis=1)
    picked = mm(dense, (row == wanted).astype(BF16))
    lane = iota((SIZE, 128), 1)
    copies[4].wait()
    by_real = jnp.zeros((SIZE, 128), F32)
    by_imag = jnp.zeros((SIZE, 128), F32)
    for k in range(ENTRIES):
        one = jnp.where((lane & 63) == k, picked, 0.0).astype(BF16)
        by_real += mm(transfer[k, 0], one)
        by_imag += mm(transfer[k, 1], one)
    local = combine(by_real, by_imag)
    for shift in (8, 4, 2, 1):
        local = local + pltpu.roll(local, 128 - shift, 1)
    local = jnp.where((lane & 63) == 0, local, 0.0).astype(BF16)
    copies[3].wait()
    local = combine(mm(own_op[0], local), mm(own_op[1], local)).astype(BF16)
    place = parent_columns()
    for level, near in ((2, low_near), (1, mid_near)):
        parents = mm(local, place).astype(BF16)
        copies[level].wait()
        by_real = jnp.zeros((SIZE, 128), F32)
        by_imag = jnp.zeros((SIZE, 128), F32)
        for c in range(OCTANTS):
            one = parents[:, 128 * c : 128 * (c + 1)]
            by_real += mm(down[level, c, 0], one)
            by_imag += mm(down[level, c, 1], one)
        local = (combine(by_real, by_imag) + near[...]).astype(BF16)
    copies[0].wait()
    row = iota((128, 1024), 0)
    col = iota((128, 1024), 1)
    by_real = jnp.zeros((SIZE, 1024), F32)
    by_imag = jnp.zeros((SIZE, 1024), F32)
    child = col & (FINE - 1)
    source = (col >> 9) * HALF + (child >> 3)
    for c in range(OCTANTS):
        spread = (row == jnp.where((child & 7) == c, source, -1)).astype(BF16)
        parents = mm(local, spread).astype(BF16)
        by_real += mm(down[0, c, 0], parents)
        by_imag += mm(down[0, c, 1], parents)
    real = by_real[:, :FINE] - by_imag[:, FINE:]
    imag = by_real[:, FINE:] + by_imag[:, :FINE]
    out[0, :, :REACH] = fine_near_a[0] + real[:, :REACH]
    out[0, :, REACH:] = fine_near_b[0] + real[:, REACH:]
    out[1, :, :REACH] = fine_near_a[1] + imag[:, :REACH]
    out[1, :, REACH:] = fine_near_b[1] + imag[:, REACH:]


def shape(dims, dtype):
    return jax.ShapeDtypeStruct(dims, dtype)


VMEM = pl.BlockSpec(memory_space=pltpu.VMEM)
SMEM = pl.BlockSpec(memory_space=pltpu.SMEM)
ANY = pl.BlockSpec(memory_space=pl.ANY)
INTERPRET = False


def call(kernel, ins, outs, scratch, flops, limit=40):
    return pl.pallas_call(
        kernel,
        in_specs=ins,
        out_specs=[VMEM] * len(outs),
        out_shape=outs,
        scratch_shapes=scratch,
        compiler_params=pltpu.CompilerParams(vmem_limit_bytes=limit << 20),
        cost_estimate=pl.CostEstimate(flops=flops, bytes_accessed=8 << 20, transcendentals=0),
        interpret=INTERPRET,
    )


def body(
    check_field, to_equiv, upward_ops, downward_ops, transfer_ops, list_fine, list_mid, list_low, list_top
):
    axes = ("row", "col")
    rows, cols = lax.axis_size("row"), lax.axis_size("col")
    count = rows * cols
    position = lax.axis_index(axes).astype(jnp.int32).reshape(1)
    own_col = lax.axis_index("col").astype(jnp.int32).reshape(1)
    octant_ops = (2, SIZE, SIZE)
    to_left, to_right, top = call(
        up_kernel,
        [SMEM, VMEM, VMEM, ANY],
        [shape((2 * SIZE, 384), BF16), shape((2 * SIZE, 384), BF16), shape((1, 512), F32)],
        [
            pltpu.VMEM((3, OCTANTS) + octant_ops, BF16),
            pltpu.VMEM(octant_ops, BF16),
            pltpu.SemaphoreType.DMA((4,)),
        ],
        4 << 30,
        60,
    )(own_col, check_field, to_equiv, upward_ops)
    from_left = lax.ppermute(to_right, axes, [(i, (i + 1) % count) for i in range(count)])
    from_right = lax.ppermute(to_left, axes, [(i, (i - 1) % count) for i in range(count)])
    def small(ride):
        return call(
            small_kernel,
            [SMEM] + [VMEM] * 7 + [ANY],
            [shape(ride.shape, BF16), shape((SIZE, 128), F32), shape((SIZE, 128), F32)],
            [pltpu.VMEM((2, ENTRIES) + octant_ops, BF16), pltpu.SemaphoreType.DMA((2,))],
            4 << 30,
        )(position, ride, from_left, from_right, to_left, to_right, list_mid.T, list_low.T, transfer_ops)

    def fine(half, ride):
        around = (from_left, to_left, to_right) if half == 0 else (to_left, to_right, from_right)
        return call(
            functools.partial(fine_kernel, half),
            [SMEM] + [VMEM] * 5 + [ANY],
            [shape(ride.shape, BF16), shape((2, SIZE, REACH), F32)],
            [
                pltpu.VMEM((2 * SIZE, 3 * REACH), BF16),
                pltpu.VMEM((ENTRIES,) + octant_ops, BF16),
                pltpu.SemaphoreType.DMA(()),
            ],
            10 << 30,
        )(position, ride, *around, list_fine.T[:, half * REACH : (half + 1) * REACH], transfer_ops)

    def swap(x, axis, mask):
        return lax.ppermute(x, axis, [(i, i ^ mask) for i in range(lax.axis_size(axis))])

    total = top
    for mask in (1, 2, 6):
        total = total + swap(total, "col", mask)
    tops = total.astype(BF16)
    work = [small, functools.partial(fine, 0), functools.partial(fine, 1)]
    near = []
    for step, mask in enumerate((1, 2, 6, 8, 24)):
        other = swap(tops, "row", mask) if mask < rows else None
        if step < len(work):
            tops, *parts = work[step](tops)
            near += parts
        if other is not None:
            tops = jnp.concatenate([tops, other], axis=0)
    mid, low, fine_a, fine_b = near
    own_row = lax.axis_index("row").astype(jnp.int32).reshape(1)
    own_list = lax.dynamic_slice_in_dim(list_top, lax.axis_index("row"), 1, 0)
    (far,) = call(
        down_kernel,
        [SMEM, SMEM] + [VMEM] * 6 + [ANY, ANY],
        [shape((2, SIZE, FINE), F32)],
        [
            pltpu.VMEM((ENTRIES,) + octant_ops, BF16),
            pltpu.VMEM((3, OCTANTS) + octant_ops, BF16),
            pltpu.VMEM(octant_ops, BF16),
            pltpu.SemaphoreType.DMA((5,)),
        ],
        8 << 30,
    )(own_col, own_row, tops, own_list, fine_a, fine_b, mid, low, transfer_ops, downward_ops)
    return far


def solution(mesh):
    split = P(None, None, ("row", "col"))
    lists = P(("row", "col"), None)
    return jax.shard_map(
        body,
        mesh=mesh,
        in_specs=(split, P(), P(), P(), P(), lists, lists, lists, P()),
        out_specs=split,
        check_vma=False,
    )
```

```python
import functools

import jax
import jax.numpy as jnp
from jax import lax
from jax.experimental import pallas as pl
from jax.experimental.pallas import tpu as pltpu
from jax.sharding import PartitionSpec as P

SIZE = 152
HALF = 64
FINE = 512
REACH = 256
ENTRIES = 16
OCTANTS = 8
BF16 = jnp.bfloat16
F32 = jnp.float32


def mm(a, b):
    return jnp.dot(a, b, preferred_element_type=F32)


def iota(shape, dim):
    return lax.broadcasted_iota(jnp.int32, shape, dim)


def combine(by_real, by_imag):
    turned = pltpu.roll(by_imag, HALF, 1)
    return by_real + jnp.where(iota(turned.shape, 1) < HALF, -turned, turned)


def child_columns():
    row = iota((128, 1024), 0)
    col = iota((128, 1024), 1)
    octant, lane = col >> 7, col & 127
    box = (lane & 63) * 8 + octant
    wanted = jnp.where(box < HALF, (lane & HALF) + box, -1)
    return (row == wanted).astype(BF16)


def parent_columns():
    row = iota((128, 1024), 0)
    col = iota((128, 1024), 1)
    octant, lane = col >> 7, col & 127
    box = lane & 63
    wanted = jnp.where((box & 7) == octant, (lane & HALF) + (box >> 3), -1)
    return (row == wanted).astype(BF16)


def regroup(first, second):
    low = iota(first.shape, 1) < HALF
    return (
        jnp.where(low, first, pltpu.roll(second, HALF, 1)),
        jnp.where(low, pltpu.roll(first, HALF, 1), second),
    )


def apply_each(ops, columns, count):
    by_real = jnp.zeros((SIZE, 128), F32)
    by_imag = jnp.zeros((SIZE, 128), F32)
    for c in range(count):
        one = columns(c)
        by_real += mm(ops[c, 0], one)
        by_imag += mm(ops[c, 1], one)
    return combine(by_real, by_imag)


def tile(array, index):
    return array[:, 128 * index : 128 * (index + 1)]


def up_kernel(
    col_ref, check_hbm, equiv_hbm, ops_hbm, to_left, to_right, top, check, equiv, ops, own_op, sems
):
    first = [
        pltpu.make_async_copy(equiv_hbm, equiv, sems.at[4]),
        pltpu.make_async_copy(check_hbm, check, sems.at[5]),
    ]
    copies = [
        pltpu.make_async_copy(ops_hbm.at[level], ops.at[level], sems.at[level])
        for level in range(3)
    ]
    copies.append(pltpu.make_async_copy(ops_hbm.at[3, col_ref[0]], own_op, sems.at[3]))
    for copy in first + copies:
        copy.start()
    row = iota((FINE, FINE), 0)
    col = iota((FINE, FINE), 1)
    by_octant = (row == (col & 63) * 8 + (col >> 6)).astype(BF16)
    pick = child_columns()
    for copy in first:
        copy.wait()
    field = jnp.concatenate([check[0], check[1]], axis=1)
    by_real = mm(equiv[0], field)
    by_imag = mm(equiv[1], field)
    real = by_real[:, :FINE] - by_imag[:, FINE:]
    imag = by_real[:, FINE:] + by_imag[:, :FINE]
    dense = jnp.concatenate([real, imag], axis=0).astype(BF16)
    to_left[:, :REACH] = dense[:, :REACH]
    to_right[:, :REACH] = dense[:, REACH:]
    ordered = mm(dense, by_octant)
    children = []
    for pair in range(OCTANTS // 2):
        children += regroup(tile(ordered[:SIZE], pair), tile(ordered[SIZE:], pair))
    children = [child.astype(BF16) for child in children]
    packed = []
    for level in range(3):
        copies[level].wait()
        packed.append(apply_each(ops.at[level], lambda c: children[c], OCTANTS).astype(BF16))
        if level < 2:
            spread = mm(packed[level], pick).astype(BF16)
            children = [tile(spread, c) for c in range(OCTANTS)]
    both = jnp.concatenate([packed[0].astype(F32), packed[1].astype(F32)], axis=0).astype(BF16)
    to_left[:, REACH:] = both
    to_right[:, REACH:] = both
    copies[3].wait()
    part = combine(mm(own_op[0], packed[2]), mm(own_op[1], packed[2]))
    flat = jnp.transpose(jnp.concatenate([part, jnp.zeros((104, 128), F32)], axis=0))
    top[:, :256] = flat[0:1, :]
    top[:, 256:] = flat[HALF : HALF + 1, :]


def load_kernel(
    col_ref, ride, transfer_hbm, down_hbm, ride_out, transfer, down, own_op, sems
):
    ride_out[...] = ride[...]
    copies = [
        pltpu.make_async_copy(transfer_hbm.at[3], transfer, sems.at[0]),
        pltpu.make_async_copy(down_hbm.at[3, col_ref[0]], own_op, sems.at[1]),
    ]
    for level in range(3):
        copies.append(
            pltpu.make_async_copy(down_hbm.at[level], down.at[level], sems.at[2 + level])
        )
    for copy in copies:
        copy.start()
    for copy in copies:
        copy.wait()


def translate_packed(around, codes, targets, ops, copy):
    select = jnp.concatenate(
        [(codes == targets[k : k + 1, :]).astype(BF16) for k in range(ENTRIES)], axis=1
    )
    picked = mm(around, select).astype(BF16)
    copy.wait()
    return apply_each(ops, lambda k: tile(picked, k), ENTRIES)


def low_kernel(
    start_ref, ride, from_left, from_right, own, low_t, ops_hbm, ride_out, out, ops, sem
):
    ride_out[...] = ride[...]
    copy = pltpu.make_async_copy(ops_hbm.at[2], ops, sem)
    copy.start()
    lows = [ref[:, REACH:].astype(F32)[SIZE:] for ref in (own, from_left, from_right)]
    around = (lows[0] + pltpu.roll(lows[1], 8, 1) + pltpu.roll(lows[2], 16, 1)).astype(BF16)
    row = iota((128, 128), 0)
    lane = row & 63
    place = jnp.where(lane < 8, lane, jnp.where(lane < 16, lane - 16, lane - 8))
    codes = jnp.where(lane < 24, (row >> 6) * 1024 + place, -(1 << 20))
    index = low_t[...] - start_ref[0] * 8
    pad = jnp.full((ENTRIES, HALF - 8), -(1 << 19), jnp.int32)
    targets = jnp.concatenate([index, pad, index + 1024, pad], axis=1)
    out[...] = translate_packed(around, codes, targets, ops, copy)


def mid_kernel(
    start_ref, ride, from_left, from_right, own, mid_t, ops_hbm, ride_out, out, ops, sem
):
    ride_out[...] = ride[...]
    copy = pltpu.make_async_copy(ops_hbm.at[1], ops, sem)
    copy.start()
    mids = [ref[:, REACH:].astype(F32)[:SIZE] for ref in (from_left, own, from_right)]
    around = jnp.concatenate(mids, axis=1).astype(BF16)
    row = iota((384, 128), 0)
    codes = ((row >> 6) & 1) * 1024 + (row & 63) + ((row >> 7) - 1) * HALF
    index = mid_t[...] - start_ref[0] * HALF
    targets = jnp.concatenate([index, index + 1024], axis=1)
    out[...] = translate_packed(around, codes, targets, ops, copy)


def fine_kernel(
    half, start_ref, ride, before, first, second, fine_t, ops_hbm, ride_out, out, window, picked, ops, sem
):
    ride_out[...] = ride[...]
    copy = pltpu.make_async_copy(ops_hbm.at[0], ops, sem)
    copy.start()
    window[:, :REACH] = before[:, :REACH]
    window[:, REACH : 2 * REACH] = first[:, :REACH]
    window[:, 2 * REACH :] = second[:, :REACH]
    index = fine_t[:, half * REACH : (half + 1) * REACH] - (start_ref[0] * FINE + (half - 1) * REACH)
    row = iota((3 * REACH, REACH), 0)
    for k in range(ENTRIES):
        select = (row == index[k : k + 1, :]).astype(BF16)
        both = mm(window[...], select)
        picked[k, :, :REACH] = both[:SIZE].astype(BF16)
        picked[k, :, REACH:] = both[SIZE:].astype(BF16)
    copy.wait()
    by_real = jnp.zeros((SIZE, FINE), F32)
    by_imag = jnp.zeros((SIZE, FINE), F32)
    for k in range(ENTRIES):
        by_real += mm(ops[k, 0], picked[k])
        by_imag += mm(ops[k, 1], picked[k])
    out[0] = by_real[:, :REACH] - by_imag[:, REACH:]
    out[1] = by_real[:, REACH:] + by_imag[:, :REACH]


def down_kernel(
    own_ref, tops, own_list, fine_near_a, fine_near_b, mid_near, low_near, transfer, down, own_op, out
):
    gap = jnp.zeros((HALF - tops.shape[0], 256), F32)
    wide = tops[...].astype(F32)
    rows = jnp.concatenate([wide[:, :256], gap, wide[:, 256:], gap], axis=0)
    dense = jnp.transpose(rows)[:SIZE].astype(BF16)
    listed = own_list[...] ^ own_ref[0]
    listed = listed ^ ((listed >> 1) & 0b01010)
    pad = jnp.full((1, HALF - ENTRIES), -(1 << 19), jnp.int32)
    wanted = jnp.concatenate([listed, pad, listed + HALF, pad], axis=1)
    picked = mm(dense, (iota((128, 128), 0) == wanted).astype(BF16))
    entry = iota((SIZE, 128), 1) & 63
    local = apply_each(transfer, lambda k: jnp.where(entry == k, picked, 0.0).astype(BF16), ENTRIES)
    for shift in (8, 4, 2, 1):
        local = local + pltpu.roll(local, 128 - shift, 1)
    local = jnp.where(entry == 0, local, 0.0).astype(BF16)
    local = combine(mm(own_op[0], local), mm(own_op[1], local)).astype(BF16)
    place = parent_columns()
    for level, near in ((2, low_near), (1, mid_near)):
        parents = mm(local, place).astype(BF16)
        local = apply_each(down.at[level], lambda c: tile(parents, c), OCTANTS) + near[...]
        local = local.astype(BF16)
    real, imag = [], []
    for pair in range(OCTANTS // 2):
        terms = [
            combine(mm(down[0, c, 0], local), mm(down[0, c, 1], local))
            for c in (2 * pair, 2 * pair + 1)
        ]
        one_real, one_imag = regroup(*terms)
        real.append(one_real)
        imag.append(one_imag)
    both = jnp.concatenate([jnp.concatenate(real, axis=1), jnp.concatenate(imag, axis=1)], axis=0)
    high = both.astype(BF16)
    low = (both - high.astype(F32)).astype(BF16)
    row = iota((FINE, FINE), 0)
    col = iota((FINE, FINE), 1)
    place = (row == (col & 7) * HALF + (col >> 3)).astype(BF16)
    far = mm(high, place) + mm(low, place)
    out[0, :, :REACH] = fine_near_a[0] + far[:SIZE, :REACH]
    out[0, :, REACH:] = fine_near_b[0] + far[:SIZE, REACH:]
    out[1, :, :REACH] = fine_near_a[1] + far[SIZE:, :REACH]
    out[1, :, REACH:] = fine_near_b[1] + far[SIZE:, REACH:]


def shape(dims, dtype):
    return jax.ShapeDtypeStruct(dims, dtype)


VMEM = pl.BlockSpec(memory_space=pltpu.VMEM)
SMEM = pl.BlockSpec(memory_space=pltpu.SMEM)
HBM = pl.BlockSpec(memory_space=pltpu.HBM)
INTERPRET = False


def in_hbm(x):
    return x if INTERPRET else pltpu.with_memory_space_constraint(x, pltpu.HBM)


def on_chip(dims, dtype):
    return shape(dims, dtype) if INTERPRET else pltpu.VMEM(dims, dtype)


def call(kernel, ins, outs, scratch, flops, limit=40):
    return pl.pallas_call(
        kernel,
        in_specs=ins,
        out_specs=[VMEM] * len(outs),
        out_shape=outs,
        scratch_shapes=scratch,
        compiler_params=pltpu.CompilerParams(vmem_limit_bytes=limit << 20),
        cost_estimate=pl.CostEstimate(flops=flops, bytes_accessed=8 << 20, transcendentals=0),
        interpret=INTERPRET,
    )


def body(
    check_field, to_equiv, upward_ops, downward_ops, transfer_ops, list_fine, list_mid, list_low, list_top
):
    axes = ("row", "col")
    rows, cols = lax.axis_size("row"), lax.axis_size("col")
    count = rows * cols
    position = lax.axis_index(axes).astype(jnp.int32).reshape(1)
    own_col = lax.axis_index("col").astype(jnp.int32).reshape(1)
    own_row = lax.axis_index("row").astype(jnp.int32).reshape(1)
    check_field, to_equiv, upward_ops, downward_ops, transfer_ops = [
        in_hbm(x) for x in (check_field, to_equiv, upward_ops, downward_ops, transfer_ops)
    ]
    octant_ops = (2, SIZE, SIZE)
    to_left, to_right, top = call(
        up_kernel,
        [SMEM, HBM, HBM, HBM],
        [shape((2 * SIZE, 384), BF16), shape((2 * SIZE, 384), BF16), shape((1, 512), F32)],
        [
            pltpu.VMEM((2, SIZE, FINE), BF16),
            pltpu.VMEM(octant_ops, BF16),
            pltpu.VMEM((3, OCTANTS) + octant_ops, BF16),
            pltpu.VMEM(octant_ops, BF16),
            pltpu.SemaphoreType.DMA((6,)),
        ],
        4 << 30,
    )(own_col, check_field, to_equiv, upward_ops)
    from_left = lax.ppermute(to_right, axes, [(i, (i + 1) % count) for i in range(count)])
    from_right = lax.ppermute(to_left, axes, [(i, (i - 1) % count) for i in range(count)])

    def load(ride):
        return call(
            load_kernel,
            [SMEM, VMEM, HBM, HBM],
            [
                shape(ride.shape, ride.dtype),
                on_chip((ENTRIES,) + octant_ops, BF16),
                on_chip((3, OCTANTS) + octant_ops, BF16),
                on_chip(octant_ops, BF16),
            ],
            [pltpu.SemaphoreType.DMA((5,))],
            4 << 30,
        )(own_col, ride, transfer_ops, downward_ops)

    def small(kernel, listed, ride):
        return call(
            kernel,
            [SMEM] + [VMEM] * 5 + [HBM],
            [shape(ride.shape, ride.dtype), shape((SIZE, 128), F32)],
            [pltpu.VMEM((ENTRIES,) + octant_ops, BF16), pltpu.SemaphoreType.DMA(())],
            4 << 30,
        )(position, ride, from_left, from_right, to_left, listed.T, transfer_ops)

    def fine(half, ride):
        around = (from_left, to_left, to_right) if half == 0 else (to_left, to_right, from_right)
        return call(
            functools.partial(fine_kernel, half),
            [SMEM] + [VMEM] * 5 + [HBM],
            [shape(ride.shape, ride.dtype), shape((2, SIZE, REACH), F32)],
            [
                pltpu.VMEM((2 * SIZE, 3 * REACH), BF16),
                pltpu.VMEM((ENTRIES, SIZE, FINE), BF16),
                pltpu.VMEM((ENTRIES,) + octant_ops, BF16),
                pltpu.SemaphoreType.DMA(()),
            ],
            6 << 30,
        )(position, ride, *around, list_fine.T, transfer_ops)

    def swap(x, axis, mask):
        return lax.ppermute(x, axis, [(i, i ^ mask) for i in range(lax.axis_size(axis))])

    work = {
        1: load,
        2: functools.partial(fine, 0),
        3: functools.partial(fine, 1),
        4: functools.partial(small, mid_kernel, list_mid),
        5: functools.partial(small, low_kernel, list_low),
    }
    done = {}
    total = top
    for step, mask in enumerate((1, 2, 6, 1, 2, 6, 8, 24)):
        axis = "col" if step < 3 else "row"
        other = swap(total, axis, mask) if axis == "col" or mask < rows else None
        if step in work:
            total, *done[step] = work[step](total)
        if axis == "col":
            total = total + other
        elif other is not None:
            total = jnp.concatenate([total, other], axis=0)
        if step == 2:
            total = total.astype(BF16)
    own_list = lax.dynamic_slice_in_dim(list_top, lax.axis_index("row"), 1, 0)
    (far,) = call(
        down_kernel,
        [SMEM] + [VMEM] * 9,
        [shape((2, SIZE, FINE), F32)],
        [],
        8 << 30,
    )(own_row, total, own_list, *done[2], *done[3], *done[4], *done[5], *done[1])
    return far


def solution(mesh):
    split = P(None, None, ("row", "col"))
    lists = P(("row", "col"), None)
    return jax.shard_map(
        body,
        mesh=mesh,
        in_specs=(split, P(), P(), P(), P(), lists, lists, lists, P()),
        out_specs=split,
        check_vma=False,
    )
```

```python
import functools

import jax
import jax.numpy as jnp
from jax import lax
from jax.experimental import pallas as pl
from jax.experimental.pallas import tpu as pltpu
from jax.sharding import PartitionSpec as P

SIZE = 152
HALF = 64
FINE = 512
REACH = 256
ENTRIES = 16
GROUP = 8
OCTANTS = 8
BF16 = jnp.bfloat16
F32 = jnp.float32


def mm(a, b):
    return jnp.dot(a, b, preferred_element_type=F32)


def iota(shape, dim):
    return lax.broadcasted_iota(jnp.int32, shape, dim)


def combine(by_real, by_imag):
    turned = pltpu.roll(by_imag, HALF, 1)
    return by_real + jnp.where(iota(turned.shape, 1) < HALF, -turned, turned)


def child_columns():
    row = iota((128, 1024), 0)
    col = iota((128, 1024), 1)
    octant, lane = col >> 7, col & 127
    box = (lane & 63) * 8 + octant
    wanted = jnp.where(box < HALF, (lane & HALF) + box, -1)
    return (row == wanted).astype(BF16)


def parent_columns():
    row = iota((128, 1024), 0)
    col = iota((128, 1024), 1)
    octant, lane = col >> 7, col & 127
    box = lane & 63
    wanted = jnp.where((box & 7) == octant, (lane & HALF) + (box >> 3), -1)
    return (row == wanted).astype(BF16)


def regroup(first, second):
    low = iota(first.shape, 1) < HALF
    return (
        jnp.where(low, first, pltpu.roll(second, HALF, 1)),
        jnp.where(low, pltpu.roll(first, HALF, 1), second),
    )


def apply_each(ops, columns, count):
    by_real = jnp.zeros((SIZE, 128), F32)
    by_imag = jnp.zeros((SIZE, 128), F32)
    for c in range(count):
        one = columns(c)
        by_real += mm(ops[c, 0], one)
        by_imag += mm(ops[c, 1], one)
    return combine(by_real, by_imag)


def tile(array, index):
    return array[:, 128 * index : 128 * (index + 1)]


def up_kernel(
    check_hbm, equiv_hbm, ops_hbm, to_left, to_right, top, check, equiv, ops, own_op, sems
):
    first = [
        pltpu.make_async_copy(equiv_hbm, equiv, sems.at[4]),
        pltpu.make_async_copy(check_hbm, check, sems.at[5]),
    ]
    copies = [
        pltpu.make_async_copy(ops_hbm.at[level], ops.at[level], sems.at[level])
        for level in range(3)
    ]
    copies.append(pltpu.make_async_copy(ops_hbm.at[3, lax.axis_index("col")], own_op, sems.at[3]))
    for copy in first + copies:
        copy.start()
    row = iota((FINE, FINE), 0)
    col = iota((FINE, FINE), 1)
    by_octant = (row == (col & 63) * 8 + (col >> 6)).astype(BF16)
    pick = child_columns()
    for copy in first:
        copy.wait()
    field = jnp.concatenate([check[0], check[1]], axis=1)
    by_real = mm(equiv[0], field)
    by_imag = mm(equiv[1], field)
    real = by_real[:, :FINE] - by_imag[:, FINE:]
    imag = by_real[:, FINE:] + by_imag[:, :FINE]
    dense = jnp.concatenate([real, imag], axis=0).astype(BF16)
    to_left[:, :REACH] = dense[:, :REACH]
    to_right[:, :REACH] = dense[:, REACH:]
    ordered = mm(dense, by_octant)
    children = []
    for pair in range(OCTANTS // 2):
        children += regroup(tile(ordered[:SIZE], pair), tile(ordered[SIZE:], pair))
    children = [child.astype(BF16) for child in children]
    packed = []
    for level in range(3):
        copies[level].wait()
        packed.append(apply_each(ops.at[level], lambda c: children[c], OCTANTS).astype(BF16))
        if level < 2:
            spread = mm(packed[level], pick).astype(BF16)
            children = [tile(spread, c) for c in range(OCTANTS)]
    both = jnp.concatenate([packed[0].astype(F32), packed[1].astype(F32)], axis=0).astype(BF16)
    to_left[:, REACH:] = both
    to_right[:, REACH:] = both
    copies[3].wait()
    part = combine(mm(own_op[0], packed[2]), mm(own_op[1], packed[2]))
    flat = jnp.transpose(jnp.concatenate([part, jnp.zeros((104, 128), F32)], axis=0))
    top[:, :256] = flat[0:1, :]
    top[:, 256:] = flat[HALF : HALF + 1, :]


def load_kernel(ride, transfer_hbm, ride_out, transfer, sem):
    ride_out[...] = ride[...]
    copy = pltpu.make_async_copy(transfer_hbm.at[3], transfer, sem)
    copy.start()
    copy.wait()


def device_position():
    return lax.axis_index("row") * lax.axis_size("col") + lax.axis_index("col")


def translate_packed(around, codes, targets, ops, copies):
    select = jnp.concatenate(
        [(codes == targets[k : k + 1, :]).astype(BF16) for k in range(ENTRIES)], axis=1
    )
    picked = mm(around, select).astype(BF16)
    by_real = jnp.zeros((SIZE, 128), F32)
    by_imag = jnp.zeros((SIZE, 128), F32)
    for k in range(ENTRIES):
        if k % GROUP == 0:
            copies[k // GROUP].wait()
        by_real += mm(ops[k, 0], tile(picked, k))
        by_imag += mm(ops[k, 1], tile(picked, k))
    return combine(by_real, by_imag)


def start_copies(ops_hbm, level, ops, sems):
    copies = []
    for group in range(ENTRIES // GROUP):
        part = pl.ds(group * GROUP, GROUP)
        copies.append(pltpu.make_async_copy(ops_hbm.at[level, part], ops.at[part], sems.at[group]))
        copies[group].start()
    return copies


def low_kernel(ride, from_left, from_right, own, low_list, ops_hbm, ride_out, out, ops, sems):
    ride_out[...] = ride[...]
    copies = start_copies(ops_hbm, 2, ops, sems)
    lows = [ref[:, REACH:].astype(F32)[SIZE:] for ref in (own, from_left, from_right)]
    around = (lows[0] + pltpu.roll(lows[1], 8, 1) + pltpu.roll(lows[2], 16, 1)).astype(BF16)
    row = iota((128, 128), 0)
    lane = row & 63
    place = jnp.where(lane < 8, lane, jnp.where(lane < 16, lane - 16, lane - 8))
    codes = jnp.where(lane < 24, (row >> 6) * 1024 + place, -(1 << 20)).astype(F32)
    index = (low_list[...] - device_position() * 8).astype(F32)
    listed = jnp.transpose(jnp.concatenate([index, jnp.zeros((8, 112), F32)], axis=1))[:ENTRIES]
    pad = jnp.full((ENTRIES, HALF - 8), -(1 << 19), F32)
    targets = jnp.concatenate([listed, pad, listed + 1024, pad], axis=1)
    out[...] = translate_packed(around, codes, targets, ops, copies)


def mid_kernel(ride, from_left, from_right, own, mid_t, ops_hbm, ride_out, out, ops, sems):
    ride_out[...] = ride[...]
    copies = start_copies(ops_hbm, 1, ops, sems)
    mids = [ref[:, REACH:].astype(F32)[:SIZE] for ref in (from_left, own, from_right)]
    around = jnp.concatenate(mids, axis=1).astype(BF16)
    row = iota((384, 128), 0)
    codes = ((row >> 6) & 1) * 1024 + (row & 63) + ((row >> 7) - 1) * HALF
    index = mid_t[...] - device_position() * HALF
    targets = jnp.concatenate([index, index + 1024], axis=1)
    out[...] = translate_packed(around, codes, targets, ops, copies)


def fine_kernel(part, ride, before, first, second, fine_t, ops_hbm, *refs):
    half, group = part
    earlier, (ride_out, out, window, picked, ops, sem) = refs[:-6], refs[-6:]
    ride_out[...] = ride[...]
    begin = group * GROUP
    copy = pltpu.make_async_copy(ops_hbm.at[0, pl.ds(begin, GROUP)], ops, sem)
    copy.start()
    window[:, :REACH] = before[:, :REACH]
    window[:, REACH : 2 * REACH] = first[:, :REACH]
    window[:, 2 * REACH :] = second[:, :REACH]
    index = fine_t[begin : begin + GROUP, half * REACH : (half + 1) * REACH]
    index = index - (device_position() * FINE + (half - 1) * REACH)
    row = iota((3 * REACH, REACH), 0)
    for k in range(GROUP):
        select = (row == index[k : k + 1, :]).astype(BF16)
        both = mm(window[...], select)
        picked[k, :, :REACH] = both[:SIZE].astype(BF16)
        picked[k, :, REACH:] = both[SIZE:].astype(BF16)
    copy.wait()
    by_real = jnp.zeros((SIZE, FINE), F32)
    by_imag = jnp.zeros((SIZE, FINE), F32)
    for k in range(GROUP):
        by_real += mm(ops[k, 0], picked[k])
        by_imag += mm(ops[k, 1], picked[k])
    real = by_real[:, :REACH] - by_imag[:, REACH:]
    imag = by_real[:, REACH:] + by_imag[:, :REACH]
    if earlier:
        real += earlier[0][0]
        imag += earlier[0][1]
    out[0] = real
    out[1] = imag


def down_kernel(
    tops, others, top_list, fine_a_hbm, fine_b_hbm, mid_near, low_near, transfer, down_hbm,
    out_hbm, out, near, down, own_op, sems,
):
    copies = [
        pltpu.make_async_copy(down_hbm.at[level], down.at[level], sems.at[level])
        for level in range(3)
    ]
    copies.append(pltpu.make_async_copy(down_hbm.at[3, lax.axis_index("col")], own_op, sems.at[3]))
    near_copies = [
        pltpu.make_async_copy(hbm, near.at[half], sems.at[4 + half])
        for half, hbm in enumerate((fine_a_hbm, fine_b_hbm))
    ]
    for copy in [copies[3], copies[2], copies[1], copies[0]] + near_copies:
        copy.start()
    wide = jnp.concatenate([tops[...].astype(F32), others[...].astype(F32)], axis=0)
    gap = jnp.zeros((HALF - wide.shape[0], 256), F32)
    rows = jnp.concatenate([wide[:, :256], gap, wide[:, 256:], gap], axis=0)
    dense = jnp.transpose(rows)[:SIZE].astype(BF16)
    own_row = lax.axis_index("row")
    place = top_list[...] ^ own_row
    place = place ^ ((place >> 1) & 0b01010)
    mine = iota(place.shape, 1) == own_row
    listed = jnp.sum(jnp.where(mine, place.astype(F32), 0.0), axis=1, keepdims=True)
    pad = jnp.full((HALF - ENTRIES, 1), -1.0, F32)
    wanted = jnp.concatenate([listed, pad, listed + HALF, pad], axis=0)
    select = (iota((128, 128), 1).astype(F32) == wanted).astype(BF16)
    picked = lax.dot_general(dense, select, (((1,), (1,)), ((), ())), preferred_element_type=F32)
    entry = iota((SIZE, 128), 1) & 63
    local = apply_each(transfer, lambda k: jnp.where(entry == k, picked, 0.0).astype(BF16), ENTRIES)
    for shift in (8, 4, 2, 1):
        local = local + pltpu.roll(local, 128 - shift, 1)
    local = jnp.where(entry == 0, local, 0.0).astype(BF16)
    copies[3].wait()
    local = combine(mm(own_op[0], local), mm(own_op[1], local)).astype(BF16)
    place = parent_columns()
    for level, at_level in ((2, low_near), (1, mid_near)):
        parents = mm(local, place).astype(BF16)
        copies[level].wait()
        local = apply_each(down.at[level], lambda c: tile(parents, c), OCTANTS) + at_level[...]
        local = local.astype(BF16)
    copies[0].wait()
    real, imag = [], []
    for pair in range(OCTANTS // 2):
        terms = [
            combine(mm(down[0, c, 0], local), mm(down[0, c, 1], local))
            for c in (2 * pair, 2 * pair + 1)
        ]
        one_real, one_imag = regroup(*terms)
        real.append(one_real)
        imag.append(one_imag)
    row = iota((FINE, FINE), 0)
    col = iota((FINE, FINE), 1)
    place = (row == (col & 7) * HALF + (col >> 3)).astype(BF16)
    for copy in near_copies:
        copy.wait()
    out_copies = []
    for part, terms in enumerate((real, imag)):
        term = jnp.concatenate(terms, axis=1)
        high = term.astype(BF16)
        low = (term - high.astype(F32)).astype(BF16)
        far = mm(high, place) + mm(low, place)
        out[part, :, :REACH] = near[0, part] + far[:, :REACH]
        out[part, :, REACH:] = near[1, part] + far[:, REACH:]
        out_copies.append(pltpu.make_async_copy(out.at[part], out_hbm.at[part], sems.at[6 + part]))
        out_copies[part].start()
    for copy in out_copies:
        copy.wait()


def shape(dims, dtype):
    return jax.ShapeDtypeStruct(dims, dtype)


VMEM = pl.BlockSpec(memory_space=pltpu.VMEM)
SMEM = pl.BlockSpec(memory_space=pltpu.SMEM)
HBM = pl.BlockSpec(memory_space=pltpu.HBM)
INTERPRET = False


def in_hbm(x):
    return x if INTERPRET else pltpu.with_memory_space_constraint(x, pltpu.HBM)


def on_chip(dims, dtype):
    return shape(dims, dtype) if INTERPRET else pltpu.VMEM(dims, dtype)


def call(kernel, ins, outs, scratch, flops, limit=16, place=VMEM):
    return pl.pallas_call(
        kernel,
        in_specs=ins,
        out_specs=[place] * len(outs),
        out_shape=outs,
        scratch_shapes=scratch,
        compiler_params=pltpu.CompilerParams(vmem_limit_bytes=limit << 20),
        cost_estimate=pl.CostEstimate(flops=flops, bytes_accessed=8 << 20, transcendentals=0),
        interpret=INTERPRET,
    )


def body(
    check_field, to_equiv, upward_ops, downward_ops, transfer_ops, list_fine, list_mid, list_low, list_top
):
    axes = ("row", "col")
    rows, cols = lax.axis_size("row"), lax.axis_size("col")
    count = rows * cols
    check_field, to_equiv, upward_ops, downward_ops, transfer_ops = [
        in_hbm(x) for x in (check_field, to_equiv, upward_ops, downward_ops, transfer_ops)
    ]
    octant_ops = (2, SIZE, SIZE)
    to_left, to_right, top = call(
        up_kernel,
        [HBM, HBM, HBM],
        [shape((2 * SIZE, 384), BF16), shape((2 * SIZE, 384), BF16), shape((1, 512), F32)],
        [
            pltpu.VMEM((2, SIZE, FINE), BF16),
            pltpu.VMEM(octant_ops, BF16),
            pltpu.VMEM((3, OCTANTS) + octant_ops, BF16),
            pltpu.VMEM(octant_ops, BF16),
            pltpu.SemaphoreType.DMA((6,)),
        ],
        4 << 30,
    )(check_field, to_equiv, upward_ops)
    from_left = lax.ppermute(to_right, axes, [(i, (i + 1) % count) for i in range(count)])
    from_right = lax.ppermute(to_left, axes, [(i, (i - 1) % count) for i in range(count)])

    def load(ride):
        return call(
            load_kernel,
            [VMEM, HBM],
            [shape(ride.shape, ride.dtype), on_chip((ENTRIES,) + octant_ops, BF16)],
            [pltpu.SemaphoreType.DMA(())],
            2 << 30,
        )(ride, transfer_ops)

    def small(kernel, listed, ride):
        return call(
            kernel,
            [VMEM] * 5 + [HBM],
            [shape(ride.shape, ride.dtype), shape((SIZE, 128), F32)],
            [pltpu.VMEM((ENTRIES,) + octant_ops, BF16), pltpu.SemaphoreType.DMA((2,))],
            3 << 30,
        )(ride, from_left, from_right, to_left, listed, transfer_ops)

    def fine(half, group, earlier, ride):
        around = (from_left, to_left, to_right) if half == 0 else (to_left, to_right, from_right)
        return call(
            functools.partial(fine_kernel, (half, group)),
            [VMEM] * 5 + [HBM] + [VMEM] * len(earlier),
            [shape(ride.shape, ride.dtype), shape((2, SIZE, REACH), F32)],
            [
                pltpu.VMEM((2 * SIZE, 3 * REACH), BF16),
                pltpu.VMEM((GROUP, SIZE, FINE), BF16),
                pltpu.VMEM((GROUP,) + octant_ops, BF16),
                pltpu.SemaphoreType.DMA(()),
            ],
            4 << 30,
        )(ride, *around, list_fine.T, transfer_ops, *earlier)

    def swap(x, axis, mask):
        return lax.ppermute(x, axis, [(i, i ^ mask) for i in range(lax.axis_size(axis))])

    work = {
        1: lambda ride: fine(0, 0, [], ride),
        2: lambda ride: fine(0, 1, done[1], ride),
        3: lambda ride: fine(1, 0, [], ride),
        4: lambda ride: fine(1, 1, done[3], ride),
        5: functools.partial(small, mid_kernel, list_mid.T),
        6: functools.partial(small, low_kernel, list_low),
        7: load,
    }
    done = {}
    total = top
    for step, mask in enumerate((1, 2, 6, 1, 2, 6, 8, 24)):
        axis = "col" if step < 3 else "row"
        other = swap(total, axis, mask) if axis == "col" or mask < rows else None
        if step in work:
            total, *done[step] = work[step](total)
        if axis == "col":
            total = total + other
        elif step < 7:
            total = total if other is None else jnp.concatenate([total, other], axis=0)
        if step == 2:
            total = total.astype(BF16)
    other = total if other is None else other
    (far,) = call(
        down_kernel,
        [VMEM] * 3 + [HBM] * 2 + [VMEM] * 3 + [HBM],
        [shape((2, SIZE, FINE), F32)],
        [
            pltpu.VMEM((2, SIZE, FINE), F32),
            pltpu.VMEM((2, 2, SIZE, REACH), F32),
            pltpu.VMEM((3, OCTANTS) + octant_ops, BF16),
            pltpu.VMEM(octant_ops, BF16),
            pltpu.SemaphoreType.DMA((8,)),
        ],
        8 << 30,
        place=HBM,
    )(
        total, other, list_top.T, in_hbm(done[2][0]), in_hbm(done[4][0]), *done[5], *done[6], *done[7],
        downward_ops,
    )
    return far


def solution(mesh):
    split = P(None, None, ("row", "col"))
    lists = P(("row", "col"), None)
    return jax.shard_map(
        body,
        mesh=mesh,
        in_specs=(split, P(), P(), P(), P(), lists, lists, lists, P()),
        out_specs=split,
        check_vma=False,
    )
```

```python
import functools

import jax
import jax.numpy as jnp
from jax import lax
from jax.experimental import pallas as pl
from jax.experimental.pallas import tpu as pltpu
from jax.sharding import PartitionSpec as P

SIZE = 152
HALF = 64
FINE = 512
REACH = 256
ENTRIES = 16
GROUP = 8
OCTANTS = 8
BF16 = jnp.bfloat16
F32 = jnp.float32


def mm(a, b):
    return jnp.dot(a, b, preferred_element_type=F32)


def iota(shape, dim):
    return lax.broadcasted_iota(jnp.int32, shape, dim)


def combine(by_real, by_imag):
    turned = pltpu.roll(by_imag, HALF, 1)
    return by_real + jnp.where(iota(turned.shape, 1) < HALF, -turned, turned)


def child_columns():
    row = iota((128, 1024), 0)
    col = iota((128, 1024), 1)
    octant, lane = col >> 7, col & 127
    box = (lane & 63) * 8 + octant
    wanted = jnp.where(box < HALF, (lane & HALF) + box, -1)
    return (row == wanted).astype(BF16)


def parent_columns():
    row = iota((128, 1024), 0)
    col = iota((128, 1024), 1)
    octant, lane = col >> 7, col & 127
    box = lane & 63
    wanted = jnp.where((box & 7) == octant, (lane & HALF) + (box >> 3), -1)
    return (row == wanted).astype(BF16)


def regroup(first, second):
    low = iota(first.shape, 1) < HALF
    return (
        jnp.where(low, first, pltpu.roll(second, HALF, 1)),
        jnp.where(low, pltpu.roll(first, HALF, 1), second),
    )


def apply_each(ops, columns, count):
    by_real = jnp.zeros((SIZE, 128), F32)
    by_imag = jnp.zeros((SIZE, 128), F32)
    for c in range(count):
        one = columns(c)
        by_real += mm(ops[c, 0], one)
        by_imag += mm(ops[c, 1], one)
    return combine(by_real, by_imag)


def tile(array, index):
    return array[:, 128 * index : 128 * (index + 1)]


def pass_on(ride, ride_out):
    def step(i, carry):
        part = pl.ds(pl.multiple_of(i * 256, 256), 256)
        ride_out[:, part] = ride[:, part]
        return carry

    lax.fori_loop(0, 2, step, 0)


def fill_places(places, row_to_col):
    def step(i, carry):
        begin = pl.multiple_of(i * 256, 256)
        row = iota((256, FINE), 0) + begin
        col = iota((256, FINE), 1)
        places[pl.ds(begin, 256), :] = (row == row_to_col(col)).astype(BF16)
        return carry

    lax.fori_loop(0, 2, step, 0)


def up_kernel(
    check_hbm, equiv_hbm, ops_hbm, to_left, to_right, top, check, equiv, ops, own_op, by_octant, sems
):
    first = [
        pltpu.make_async_copy(equiv_hbm, equiv, sems.at[4]),
        pltpu.make_async_copy(check_hbm, check, sems.at[5]),
    ]
    copies = [
        pltpu.make_async_copy(ops_hbm.at[level], ops.at[level], sems.at[level])
        for level in range(3)
    ]
    copies.append(pltpu.make_async_copy(ops_hbm.at[3, lax.axis_index("col")], own_op, sems.at[3]))
    for copy in first + copies:
        copy.start()
    fill_places(by_octant, lambda col: (col & 63) * 8 + (col >> 6))
    pick = child_columns()
    for copy in first:
        copy.wait()
    field = jnp.concatenate([check[0], check[1]], axis=1)
    by_real = mm(equiv[0], field)
    by_imag = mm(equiv[1], field)
    real = by_real[:, :FINE] - by_imag[:, FINE:]
    imag = by_real[:, FINE:] + by_imag[:, :FINE]
    dense = jnp.concatenate([real, imag], axis=0).astype(BF16)
    to_left[:, :REACH] = dense[:, :REACH]
    to_right[:, :REACH] = dense[:, REACH:]
    ordered = mm(dense, by_octant[...])
    children = []
    for pair in range(OCTANTS // 2):
        children += regroup(tile(ordered[:SIZE], pair), tile(ordered[SIZE:], pair))
    children = [child.astype(BF16) for child in children]
    packed = []
    for level in range(3):
        copies[level].wait()
        packed.append(apply_each(ops.at[level], lambda c: children[c], OCTANTS).astype(BF16))
        if level < 2:
            spread = mm(packed[level], pick).astype(BF16)
            children = [tile(spread, c) for c in range(OCTANTS)]
    both = jnp.concatenate([packed[0].astype(F32), packed[1].astype(F32)], axis=0).astype(BF16)
    to_left[:, REACH:] = both
    to_right[:, REACH:] = both
    copies[3].wait()
    part = combine(mm(own_op[0], packed[2]), mm(own_op[1], packed[2]))
    flat = jnp.transpose(jnp.concatenate([part, jnp.zeros((104, 128), F32)], axis=0))
    top[:, :256] = flat[0:1, :]
    top[:, 256:] = flat[HALF : HALF + 1, :]


def load_kernel(ride, transfer_hbm, ride_out, transfer, sem):
    copy = pltpu.make_async_copy(transfer_hbm.at[3], transfer, sem)
    copy.start()
    ride_out[...] = ride[...]
    copy.wait()


def device_position():
    return lax.axis_index("row") * lax.axis_size("col") + lax.axis_index("col")


def translate_packed(around, codes, targets, ops, copies):
    select = jnp.concatenate(
        [(codes == targets[k : k + 1, :]).astype(BF16) for k in range(ENTRIES)], axis=1
    )
    picked = mm(around, select).astype(BF16)
    by_real = jnp.zeros((SIZE, 128), F32)
    by_imag = jnp.zeros((SIZE, 128), F32)
    for k in range(ENTRIES):
        if k % GROUP == 0:
            copies[k // GROUP].wait()
        by_real += mm(ops[k, 0], tile(picked, k))
        by_imag += mm(ops[k, 1], tile(picked, k))
    return combine(by_real, by_imag)


def start_copies(ops_hbm, level, ops, sems):
    copies = []
    for group in range(ENTRIES // GROUP):
        part = pl.ds(group * GROUP, GROUP)
        copies.append(pltpu.make_async_copy(ops_hbm.at[level, part], ops.at[part], sems.at[group]))
        copies[group].start()
    return copies


def low_kernel(ride, from_left, from_right, own, low_list, ops_hbm, ride_out, out, ops, sems):
    copies = start_copies(ops_hbm, 2, ops, sems)
    pass_on(ride, ride_out)
    lows = [ref[:, REACH:].astype(F32)[SIZE:] for ref in (own, from_left, from_right)]
    around = (lows[0] + pltpu.roll(lows[1], 8, 1) + pltpu.roll(lows[2], 16, 1)).astype(BF16)
    row = iota((128, 128), 0)
    lane = row & 63
    place = jnp.where(lane < 8, lane, jnp.where(lane < 16, lane - 16, lane - 8))
    codes = jnp.where(lane < 24, (row >> 6) * 1024 + place, -(1 << 20)).astype(F32)
    index = (low_list[...] - device_position() * 8).astype(F32)
    listed = jnp.transpose(jnp.concatenate([index, jnp.zeros((8, 112), F32)], axis=1))[:ENTRIES]
    pad = jnp.full((ENTRIES, HALF - 8), -(1 << 19), F32)
    targets = jnp.concatenate([listed, pad, listed + 1024, pad], axis=1)
    out[...] = translate_packed(around, codes, targets, ops, copies)


def mid_kernel(ride, from_left, from_right, own, mid_t, ops_hbm, ride_out, out, ops, sems):
    copies = start_copies(ops_hbm, 1, ops, sems)
    pass_on(ride, ride_out)
    mids = [ref[:, REACH:].astype(F32)[:SIZE] for ref in (from_left, own, from_right)]
    around = jnp.concatenate(mids, axis=1).astype(BF16)
    row = iota((384, 128), 0)
    codes = ((row >> 6) & 1) * 1024 + (row & 63) + ((row >> 7) - 1) * HALF
    index = mid_t[...] - device_position() * HALF
    targets = jnp.concatenate([index, index + 1024], axis=1)
    out[...] = translate_packed(around, codes, targets, ops, copies)


def fine_kernel(part, ride, before, first, second, fine_t, ops_hbm, *refs):
    half, group = part
    earlier, (ride_out, out, window, picked, ops, sem) = refs[:-6], refs[-6:]
    begin = group * GROUP
    copy = pltpu.make_async_copy(ops_hbm.at[0, pl.ds(begin, GROUP)], ops, sem)
    copy.start()
    pass_on(ride, ride_out)
    window[:, :REACH] = before[:, :REACH]
    window[:, REACH : 2 * REACH] = first[:, :REACH]
    window[:, 2 * REACH :] = second[:, :REACH]
    index = fine_t[begin : begin + GROUP, half * REACH : (half + 1) * REACH]
    index = index - (device_position() * FINE + (half - 1) * REACH)
    row = iota((3 * REACH, REACH), 0)
    for k in range(GROUP):
        select = (row == index[k : k + 1, :]).astype(BF16)
        both = mm(window[...], select)
        picked[k, :, :REACH] = both[:SIZE].astype(BF16)
        picked[k, :, REACH:] = both[SIZE:].astype(BF16)
    copy.wait()
    by_real = jnp.zeros((SIZE, FINE), F32)
    by_imag = jnp.zeros((SIZE, FINE), F32)
    for k in range(GROUP):
        by_real += mm(ops[k, 0], picked[k])
        by_imag += mm(ops[k, 1], picked[k])
    real = by_real[:, :REACH] - by_imag[:, REACH:]
    imag = by_real[:, REACH:] + by_imag[:, :REACH]
    if earlier:
        real += earlier[0][0]
        imag += earlier[0][1]
    out[0] = real
    out[1] = imag


def down_kernel(
    tops, others, top_list, fine_a_hbm, fine_b_hbm, mid_near, low_near, transfer, down_hbm,
    out_hbm, out, near, down, own_op, places, sems,
):
    copies = [
        pltpu.make_async_copy(down_hbm.at[level], down.at[level], sems.at[level])
        for level in range(3)
    ]
    copies.append(pltpu.make_async_copy(down_hbm.at[3, lax.axis_index("col")], own_op, sems.at[3]))
    near_copies = [
        pltpu.make_async_copy(hbm, near.at[half], sems.at[4 + half])
        for half, hbm in enumerate((fine_a_hbm, fine_b_hbm))
    ]
    for copy in [copies[3], copies[2], copies[1], copies[0]] + near_copies:
        copy.start()
    fill_places(places, lambda col: (col & 7) * HALF + (col >> 3))
    wide = jnp.concatenate([tops[...].astype(F32), others[...].astype(F32)], axis=0)
    gap = jnp.zeros((HALF - wide.shape[0], 256), F32)
    rows = jnp.concatenate([wide[:, :256], gap, wide[:, 256:], gap], axis=0)
    dense = jnp.transpose(rows)[:SIZE].astype(BF16)
    own_row = lax.axis_index("row")
    place = top_list[...] ^ own_row
    place = place ^ ((place >> 1) & 0b01010)
    mine = iota(place.shape, 1) == own_row
    listed = jnp.sum(jnp.where(mine, place.astype(F32), 0.0), axis=1, keepdims=True)
    pad = jnp.full((HALF - ENTRIES, 1), -1.0, F32)
    wanted = jnp.concatenate([listed, pad, listed + HALF, pad], axis=0)
    select = (iota((128, 128), 1).astype(F32) == wanted).astype(BF16)
    picked = lax.dot_general(dense, select, (((1,), (1,)), ((), ())), preferred_element_type=F32)
    entry = iota((SIZE, 128), 1) & 63
    local = apply_each(transfer, lambda k: jnp.where(entry == k, picked, 0.0).astype(BF16), ENTRIES)
    for shift in (8, 4, 2, 1):
        local = local + pltpu.roll(local, 128 - shift, 1)
    local = jnp.where(entry == 0, local, 0.0).astype(BF16)
    copies[3].wait()
    local = combine(mm(own_op[0], local), mm(own_op[1], local)).astype(BF16)
    place = parent_columns()
    for level, at_level in ((2, low_near), (1, mid_near)):
        parents = mm(local, place).astype(BF16)
        copies[level].wait()
        local = apply_each(down.at[level], lambda c: tile(parents, c), OCTANTS) + at_level[...]
        local = local.astype(BF16)
    copies[0].wait()
    real, imag = [], []
    for pair in range(OCTANTS // 2):
        terms = [
            combine(mm(down[0, c, 0], local), mm(down[0, c, 1], local))
            for c in (2 * pair, 2 * pair + 1)
        ]
        one_real, one_imag = regroup(*terms)
        real.append(one_real)
        imag.append(one_imag)
    for copy in near_copies:
        copy.wait()
    out_copies = []
    for part, terms in enumerate((real, imag)):
        term = jnp.concatenate(terms, axis=1)
        high = term.astype(BF16)
        low = (term - high.astype(F32)).astype(BF16)
        far = mm(high, places[...]) + mm(low, places[...])
        out[part, :, :REACH] = near[0, part] + far[:, :REACH]
        out[part, :, REACH:] = near[1, part] + far[:, REACH:]
        out_copies.append(pltpu.make_async_copy(out.at[part], out_hbm.at[part], sems.at[6 + part]))
        out_copies[part].start()
    for copy in out_copies:
        copy.wait()


def shape(dims, dtype):
    return jax.ShapeDtypeStruct(dims, dtype)


VMEM = pl.BlockSpec(memory_space=pltpu.VMEM)
SMEM = pl.BlockSpec(memory_space=pltpu.SMEM)
HBM = pl.BlockSpec(memory_space=pltpu.HBM)
INTERPRET = False


def in_hbm(x):
    return x if INTERPRET else pltpu.with_memory_space_constraint(x, pltpu.HBM)


def on_chip(dims, dtype):
    return shape(dims, dtype) if INTERPRET else pltpu.VMEM(dims, dtype)


def off_chip(dims, dtype):
    return shape(dims, dtype) if INTERPRET else pltpu.HBM(dims, dtype)


def call(kernel, ins, outs, scratch, flops, limit=16, place=VMEM):
    return pl.pallas_call(
        kernel,
        in_specs=ins,
        out_specs=[place] * len(outs),
        out_shape=outs,
        scratch_shapes=scratch,
        compiler_params=pltpu.CompilerParams(vmem_limit_bytes=limit << 20),
        cost_estimate=pl.CostEstimate(flops=flops, bytes_accessed=8 << 20, transcendentals=0),
        interpret=INTERPRET,
    )


def body(
    check_field, to_equiv, upward_ops, downward_ops, transfer_ops, list_fine, list_mid, list_low, list_top
):
    axes = ("row", "col")
    rows, cols = lax.axis_size("row"), lax.axis_size("col")
    count = rows * cols
    check_field, to_equiv, upward_ops, downward_ops, transfer_ops = [
        in_hbm(x) for x in (check_field, to_equiv, upward_ops, downward_ops, transfer_ops)
    ]
    octant_ops = (2, SIZE, SIZE)
    to_left, to_right, top = call(
        up_kernel,
        [HBM, HBM, HBM],
        [shape((2 * SIZE, 384), BF16), shape((2 * SIZE, 384), BF16), shape((1, 512), F32)],
        [
            pltpu.VMEM((2, SIZE, FINE), BF16),
            pltpu.VMEM(octant_ops, BF16),
            pltpu.VMEM((3, OCTANTS) + octant_ops, BF16),
            pltpu.VMEM(octant_ops, BF16),
            pltpu.VMEM((FINE, FINE), BF16),
            pltpu.SemaphoreType.DMA((6,)),
        ],
        4 << 30,
    )(check_field, to_equiv, upward_ops)
    from_left = lax.ppermute(to_right, axes, [(i, (i + 1) % count) for i in range(count)])
    from_right = lax.ppermute(to_left, axes, [(i, (i - 1) % count) for i in range(count)])

    def load(ride):
        return call(
            load_kernel,
            [VMEM, HBM],
            [shape(ride.shape, ride.dtype), on_chip((ENTRIES,) + octant_ops, BF16)],
            [pltpu.SemaphoreType.DMA(())],
            8 << 30,
        )(ride, transfer_ops)

    def small(kernel, listed, ride):
        return call(
            kernel,
            [VMEM] * 5 + [HBM],
            [shape(ride.shape, ride.dtype), shape((SIZE, 128), F32)],
            [pltpu.VMEM((ENTRIES,) + octant_ops, BF16), pltpu.SemaphoreType.DMA((2,))],
            3 << 30,
        )(ride, from_left, from_right, to_left, listed, transfer_ops)

    def fine(half, group, earlier, ride):
        around = (from_left, to_left, to_right) if half == 0 else (to_left, to_right, from_right)
        return call(
            functools.partial(fine_kernel, (half, group)),
            [VMEM] * 5 + [HBM] + [VMEM] * len(earlier),
            [shape(ride.shape, ride.dtype), (off_chip if group else shape)((2, SIZE, REACH), F32)],
            [
                pltpu.VMEM((2 * SIZE, 3 * REACH), BF16),
                pltpu.VMEM((GROUP, SIZE, FINE), BF16),
                pltpu.VMEM((GROUP,) + octant_ops, BF16),
                pltpu.SemaphoreType.DMA(()),
            ],
            4 << 30,
        )(ride, *around, list_fine.T, transfer_ops, *earlier)

    def swap(x, axis, mask):
        return lax.ppermute(x, axis, [(i, i ^ mask) for i in range(lax.axis_size(axis))])

    work = {
        1: load,
        2: lambda ride: fine(0, 0, [], ride),
        3: lambda ride: fine(0, 1, done[2], ride),
        4: lambda ride: fine(1, 0, [], ride),
        5: lambda ride: fine(1, 1, done[4], ride),
        6: functools.partial(small, mid_kernel, list_mid.T),
        7: functools.partial(small, low_kernel, list_low),
    }
    done = {}
    total = top
    for step, mask in enumerate((1, 2, 6, 1, 2, 6, 8, 24)):
        axis = "col" if step < 3 else "row"
        other = swap(total, axis, mask) if axis == "col" or mask < rows else None
        if step in work:
            total, *done[step] = work[step](total)
        if axis == "col":
            total = total + other
        elif step < 7:
            total = total if other is None else jnp.concatenate([total, other], axis=0)
        if step == 2:
            total = total.astype(BF16)
    other = total if other is None else other
    (far,) = call(
        down_kernel,
        [VMEM] * 3 + [HBM] * 2 + [VMEM] * 3 + [HBM],
        [shape((2, SIZE, FINE), F32)],
        [
            pltpu.VMEM((2, SIZE, FINE), F32),
            pltpu.VMEM((2, 2, SIZE, REACH), F32),
            pltpu.VMEM((3, OCTANTS) + octant_ops, BF16),
            pltpu.VMEM(octant_ops, BF16),
            pltpu.VMEM((FINE, FINE), BF16),
            pltpu.SemaphoreType.DMA((8,)),
        ],
        8 << 30,
        place=HBM,
    )(
        total, other, list_top.T, in_hbm(done[3][0]), in_hbm(done[5][0]), *done[6], *done[7], *done[1],
        downward_ops,
    )
    return far


def solution(mesh):
    split = P(None, None, ("row", "col"))
    lists = P(("row", "col"), None)
    return jax.shard_map(
        body,
        mesh=mesh,
        in_specs=(split, P(), P(), P(), P(), lists, lists, lists, P()),
        out_specs=split,
        check_vma=False,
    )
```

```python
import functools

import jax
import jax.numpy as jnp
from jax import lax
from jax.experimental import pallas as pl
from jax.experimental.pallas import tpu as pltpu
from jax.sharding import PartitionSpec as P

SIZE = 152
HALF = 64
FINE = 512
REACH = 256
ENTRIES = 16
GROUP = 8
OCTANTS = 8
BF16 = jnp.bfloat16
F32 = jnp.float32


def mm(a, b):
    return jnp.dot(a, b, preferred_element_type=F32)


def iota(shape, dim):
    return lax.broadcasted_iota(jnp.int32, shape, dim)


def combine(by_real, by_imag):
    turned = pltpu.roll(by_imag, HALF, 1)
    return by_real + jnp.where(iota(turned.shape, 1) < HALF, -turned, turned)


def box_order(lane):
    return (lane & 7) * 8 + ((lane & 63) >> 3)


def regroup(first, second):
    low = iota(first.shape, 1) < HALF
    return (
        jnp.where(low, first, pltpu.roll(second, HALF, 1)),
        jnp.where(low, pltpu.roll(first, HALF, 1), second),
    )


def apply_each(ops, columns, count):
    by_real = jnp.zeros((SIZE, 128), F32)
    by_imag = jnp.zeros((SIZE, 128), F32)
    for c in range(count):
        one = columns(c)
        by_real += mm(ops[c, 0], one)
        by_imag += mm(ops[c, 1], one)
    return combine(by_real, by_imag)


def tile(array, index):
    return array[:, 128 * index : 128 * (index + 1)]


def pass_on(ride, ride_out):
    def step(i, carry):
        part = pl.ds(pl.multiple_of(i * 256, 256), 256)
        ride_out[:, part] = ride[:, part]
        return carry

    lax.fori_loop(0, 2, step, 0)


def fill_places(places, row_to_col):
    def step(i, carry):
        begin = pl.multiple_of(i * 256, 256)
        row = iota((256, FINE), 0) + begin
        col = iota((256, FINE), 1)
        places[pl.ds(begin, 256), :] = (row == row_to_col(col)).astype(BF16)
        return carry

    lax.fori_loop(0, 2, step, 0)


def up_kernel(
    check_hbm, equiv_hbm, ops_hbm, to_left, to_right, top, check, equiv, ops, own_op, by_octant, sems
):
    first = [
        pltpu.make_async_copy(equiv_hbm, equiv, sems.at[4]),
        pltpu.make_async_copy(check_hbm, check, sems.at[5]),
    ]
    copies = [
        pltpu.make_async_copy(ops_hbm.at[level], ops.at[level], sems.at[level])
        for level in range(3)
    ]
    copies.append(pltpu.make_async_copy(ops_hbm.at[3, lax.axis_index("col")], own_op, sems.at[3]))
    for copy in first + copies:
        copy.start()
    fill_places(by_octant, lambda col: box_order(col) * 8 + (col >> 6))
    for copy in first:
        copy.wait()
    field = jnp.concatenate([check[0], check[1]], axis=1)
    by_real = mm(equiv[0], field)
    by_imag = mm(equiv[1], field)
    real = by_real[:, :FINE] - by_imag[:, FINE:]
    imag = by_real[:, FINE:] + by_imag[:, :FINE]
    dense = jnp.concatenate([real, imag], axis=0).astype(BF16)
    to_left[:, :REACH] = dense[:, :REACH]
    to_right[:, :REACH] = dense[:, REACH:]
    ordered = mm(dense, by_octant[...])
    children = []
    for pair in range(OCTANTS // 2):
        children += regroup(tile(ordered[:SIZE], pair), tile(ordered[SIZE:], pair))
    children = [child.astype(BF16) for child in children]
    copies[0].wait()
    packed = [apply_each(ops.at[0], lambda c: children[c], OCTANTS).astype(BF16)]
    lane = iota((SIZE, 128), 1) & 63
    for level, octant, steps in ((1, lane >> 3, (32, 16, 8)), (2, lane, (4, 2, 1))):
        copies[level].wait()
        below = packed[level - 1]
        by_real = mm(ops[level, 0, 0], below)
        by_imag = mm(ops[level, 0, 1], below)
        for c in range(1, OCTANTS):
            by_real = jnp.where(octant == c, mm(ops[level, c, 0], below), by_real)
            by_imag = jnp.where(octant == c, mm(ops[level, c, 1], below), by_imag)
        dense = combine(by_real, by_imag)
        for step in steps:
            dense = dense + pltpu.roll(dense, 128 - step, 1)
        packed.append(jnp.where(lane < steps[-1], dense, 0.0).astype(BF16))
    both = jnp.concatenate([packed[0].astype(F32), packed[1].astype(F32)], axis=0).astype(BF16)
    to_left[:, REACH:] = both
    to_right[:, REACH:] = both
    copies[3].wait()
    part = combine(mm(own_op[0], packed[2]), mm(own_op[1], packed[2]))
    flat = jnp.transpose(jnp.concatenate([part, jnp.zeros((104, 128), F32)], axis=0))
    top[:, :256] = flat[0:1, :]
    top[:, 256:] = flat[HALF : HALF + 1, :]


def load_kernel(ride, transfer_hbm, ride_out, transfer, sem):
    copy = pltpu.make_async_copy(transfer_hbm.at[3], transfer, sem)
    copy.start()
    ride_out[...] = ride[...]
    copy.wait()


def device_position():
    return lax.axis_index("row") * lax.axis_size("col") + lax.axis_index("col")


def translate_packed(around, codes, targets, ops, copies):
    select = jnp.concatenate(
        [(codes == targets[k : k + 1, :]).astype(BF16) for k in range(ENTRIES)], axis=1
    )
    picked = mm(around, select).astype(BF16)
    by_real = jnp.zeros((SIZE, 128), F32)
    by_imag = jnp.zeros((SIZE, 128), F32)
    for k in range(ENTRIES):
        if k % GROUP == 0:
            copies[k // GROUP].wait()
        by_real += mm(ops[k, 0], tile(picked, k))
        by_imag += mm(ops[k, 1], tile(picked, k))
    return combine(by_real, by_imag)


def start_copies(ops_hbm, level, ops, sems):
    copies = []
    for group in range(ENTRIES // GROUP):
        part = pl.ds(group * GROUP, GROUP)
        copies.append(pltpu.make_async_copy(ops_hbm.at[level, part], ops.at[part], sems.at[group]))
        copies[group].start()
    return copies


def low_kernel(ride, from_left, from_right, own, low_list, ops_hbm, ride_out, out, ops, sems):
    copies = start_copies(ops_hbm, 2, ops, sems)
    pass_on(ride, ride_out)
    lows = [ref[:, REACH:].astype(F32)[SIZE:] for ref in (own, from_left, from_right)]
    around = (lows[0] + pltpu.roll(lows[1], 8, 1) + pltpu.roll(lows[2], 16, 1)).astype(BF16)
    row = iota((128, 128), 0)
    lane = row & 63
    place = jnp.where(lane < 8, lane, jnp.where(lane < 16, lane - 16, lane - 8))
    codes = jnp.where(lane < 24, (row >> 6) * 1024 + place, -(1 << 20)).astype(F32)
    index = (low_list[...] - device_position() * 8).astype(F32)
    listed = jnp.transpose(jnp.concatenate([index, jnp.zeros((8, 112), F32)], axis=1))[:ENTRIES]
    listed = jnp.concatenate([listed, jnp.zeros((ENTRIES, 120), F32)], axis=1).astype(BF16)
    lane = iota((128, 128), 1)
    targets = mm(listed, (iota((128, 128), 0) == (lane & 63) >> 3).astype(BF16))
    targets = targets + jnp.where(iota(targets.shape, 1) < HALF, 0.0, 1024.0)
    out[...] = translate_packed(around, codes, targets, ops, copies)


def mid_kernel(ride, from_left, from_right, own, mid_t, ops_hbm, ride_out, out, ops, sems):
    copies = start_copies(ops_hbm, 1, ops, sems)
    pass_on(ride, ride_out)
    mids = [ref[:, REACH:].astype(F32)[:SIZE] for ref in (from_left, own, from_right)]
    around = jnp.concatenate(mids, axis=1).astype(BF16)
    row = iota((384, 128), 0)
    codes = ((row >> 6) & 1) * 1024 + box_order(row) + ((row >> 7) - 1) * HALF
    index = mid_t[...] - device_position() * HALF
    targets = jnp.concatenate([index, index + 1024], axis=1)
    out[...] = translate_packed(around, codes, targets, ops, copies)


def fine_kernel(part, ride, before, first, second, fine_t, ops_hbm, *refs):
    half, group = part
    earlier, (ride_out, out, window, picked, ops, sem) = refs[:-6], refs[-6:]
    begin = group * GROUP
    copy = pltpu.make_async_copy(ops_hbm.at[0, pl.ds(begin, GROUP)], ops, sem)
    copy.start()
    pass_on(ride, ride_out)
    window[:, :REACH] = before[:, :REACH]
    window[:, REACH : 2 * REACH] = first[:, :REACH]
    window[:, 2 * REACH :] = second[:, :REACH]
    index = fine_t[begin : begin + GROUP, half * REACH : (half + 1) * REACH]
    index = index - (device_position() * FINE + (half - 1) * REACH)
    row = iota((3 * REACH, REACH), 0)
    for k in range(GROUP):
        select = (row == index[k : k + 1, :]).astype(BF16)
        both = mm(window[...], select)
        picked[k, :, :REACH] = both[:SIZE].astype(BF16)
        picked[k, :, REACH:] = both[SIZE:].astype(BF16)
    copy.wait()
    by_real = jnp.zeros((SIZE, FINE), F32)
    by_imag = jnp.zeros((SIZE, FINE), F32)
    for k in range(GROUP):
        by_real += mm(ops[k, 0], picked[k])
        by_imag += mm(ops[k, 1], picked[k])
    real = by_real[:, :REACH] - by_imag[:, REACH:]
    imag = by_real[:, REACH:] + by_imag[:, :REACH]
    if earlier:
        real += earlier[0][0]
        imag += earlier[0][1]
    out[0] = real
    out[1] = imag


def down_kernel(
    tops, others, top_list, fine_a_hbm, fine_b_hbm, mid_near, low_near, transfer, down_hbm,
    out_hbm, out, near, down, own_op, places, sems,
):
    copies = [
        pltpu.make_async_copy(down_hbm.at[level], down.at[level], sems.at[level])
        for level in range(3)
    ]
    copies.append(pltpu.make_async_copy(down_hbm.at[3, lax.axis_index("col")], own_op, sems.at[3]))
    near_copies = [
        pltpu.make_async_copy(hbm, near.at[half], sems.at[4 + half])
        for half, hbm in enumerate((fine_a_hbm, fine_b_hbm))
    ]
    for copy in [copies[3], copies[2], copies[1], copies[0]] + near_copies:
        copy.start()
    fill_places(places, lambda col: (col & 7) * HALF + (col >> 3))
    wide = jnp.concatenate([tops[...].astype(F32), others[...].astype(F32)], axis=0)
    gap = jnp.zeros((HALF - wide.shape[0], 256), F32)
    rows = jnp.concatenate([wide[:, :256], gap, wide[:, 256:], gap], axis=0)
    dense = jnp.transpose(rows)[:SIZE].astype(BF16)
    own_row = lax.axis_index("row")
    place = top_list[...] ^ own_row
    place = place ^ ((place >> 1) & 0b01010)
    mine = iota(place.shape, 1) == own_row
    listed = jnp.sum(jnp.where(mine, place.astype(F32), 0.0), axis=1, keepdims=True)
    codes = (iota((128, 128), 0) - (iota((128, 128), 1) & HALF)).astype(F32)
    select = jnp.concatenate([(codes == listed[k : k + 1, :]).astype(BF16) for k in range(ENTRIES)], axis=1)
    picked = mm(dense, select).astype(BF16)
    local = apply_each(transfer, lambda k: tile(picked, k), ENTRIES).astype(BF16)
    copies[3].wait()
    local = combine(mm(own_op[0], local), mm(own_op[1], local)).astype(BF16)
    lane = iota((SIZE, 128), 1) & 63
    for level, at_level, octant in ((2, low_near, lane >> 3), (1, mid_near, lane & 7)):
        copies[level].wait()
        by_real = mm(down[level, 0, 0], local)
        by_imag = mm(down[level, 0, 1], local)
        for c in range(1, OCTANTS):
            by_real = jnp.where(octant == c, mm(down[level, c, 0], local), by_real)
            by_imag = jnp.where(octant == c, mm(down[level, c, 1], local), by_imag)
        local = (combine(by_real, by_imag) + at_level[...]).astype(BF16)
    copies[0].wait()
    real, imag = [], []
    for pair in range(OCTANTS // 2):
        terms = [
            combine(mm(down[0, c, 0], local), mm(down[0, c, 1], local))
            for c in (2 * pair, 2 * pair + 1)
        ]
        one_real, one_imag = regroup(*terms)
        real.append(one_real)
        imag.append(one_imag)
    for copy in near_copies:
        copy.wait()
    out_copies = []
    for part, terms in enumerate((real, imag)):
        term = jnp.concatenate(terms, axis=1)
        high = term.astype(BF16)
        low = (term - high.astype(F32)).astype(BF16)
        for half in range(2):
            columns = pl.ds(half * REACH, REACH)
            place = places[:, columns]
            out[part, :, columns] = near[half, part] + mm(high, place) + mm(low, place)
            copy = pltpu.make_async_copy(
                out.at[part, :, columns], out_hbm.at[part, :, columns], sems.at[6 + 2 * part + half]
            )
            copy.start()
            out_copies.append(copy)
    for copy in out_copies:
        copy.wait()


def shape(dims, dtype):
    return jax.ShapeDtypeStruct(dims, dtype)


VMEM = pl.BlockSpec(memory_space=pltpu.VMEM)
SMEM = pl.BlockSpec(memory_space=pltpu.SMEM)
HBM = pl.BlockSpec(memory_space=pltpu.HBM)
INTERPRET = False


def in_hbm(x):
    return x if INTERPRET else pltpu.with_memory_space_constraint(x, pltpu.HBM)


def on_chip(dims, dtype):
    return shape(dims, dtype) if INTERPRET else pltpu.VMEM(dims, dtype)


def off_chip(dims, dtype):
    return shape(dims, dtype) if INTERPRET else pltpu.HBM(dims, dtype)


def call(kernel, ins, outs, scratch, flops, limit=16, place=VMEM):
    return pl.pallas_call(
        kernel,
        in_specs=ins,
        out_specs=[place] * len(outs),
        out_shape=outs,
        scratch_shapes=scratch,
        compiler_params=pltpu.CompilerParams(vmem_limit_bytes=limit << 20),
        cost_estimate=pl.CostEstimate(flops=flops, bytes_accessed=8 << 20, transcendentals=0),
        interpret=INTERPRET,
    )


def body(
    check_field, to_equiv, upward_ops, downward_ops, transfer_ops, list_fine, list_mid, list_low, list_top
):
    axes = ("row", "col")
    rows, cols = lax.axis_size("row"), lax.axis_size("col")
    count = rows * cols
    check_field, to_equiv, upward_ops, downward_ops, transfer_ops = [
        in_hbm(x) for x in (check_field, to_equiv, upward_ops, downward_ops, transfer_ops)
    ]
    octant_ops = (2, SIZE, SIZE)
    to_left, to_right, top = call(
        up_kernel,
        [HBM, HBM, HBM],
        [shape((2 * SIZE, 384), BF16), shape((2 * SIZE, 384), BF16), shape((1, 512), F32)],
        [
            pltpu.VMEM((2, SIZE, FINE), BF16),
            pltpu.VMEM(octant_ops, BF16),
            pltpu.VMEM((3, OCTANTS) + octant_ops, BF16),
            pltpu.VMEM(octant_ops, BF16),
            pltpu.VMEM((FINE, FINE), BF16),
            pltpu.SemaphoreType.DMA((6,)),
        ],
        4 << 30,
    )(check_field, to_equiv, upward_ops)
    from_left = lax.ppermute(to_right, axes, [(i, (i + 1) % count) for i in range(count)])
    from_right = lax.ppermute(to_left, axes, [(i, (i - 1) % count) for i in range(count)])

    def load(ride):
        return call(
            load_kernel,
            [VMEM, HBM],
            [shape(ride.shape, ride.dtype), on_chip((ENTRIES,) + octant_ops, BF16)],
            [pltpu.SemaphoreType.DMA(())],
            8 << 30,
        )(ride, transfer_ops)

    def small(kernel, listed, ride):
        return call(
            kernel,
            [VMEM] * 5 + [HBM],
            [shape(ride.shape, ride.dtype), shape((SIZE, 128), F32)],
            [pltpu.VMEM((ENTRIES,) + octant_ops, BF16), pltpu.SemaphoreType.DMA((2,))],
            3 << 30,
        )(ride, from_left, from_right, to_left, listed, transfer_ops)

    def fine(half, group, earlier, ride):
        around = (from_left, to_left, to_right) if half == 0 else (to_left, to_right, from_right)
        return call(
            functools.partial(fine_kernel, (half, group)),
            [VMEM] * 5 + [HBM] + [VMEM] * len(earlier),
            [shape(ride.shape, ride.dtype), (off_chip if group else shape)((2, SIZE, REACH), F32)],
            [
                pltpu.VMEM((2 * SIZE, 3 * REACH), BF16),
                pltpu.VMEM((GROUP, SIZE, FINE), BF16),
                pltpu.VMEM((GROUP,) + octant_ops, BF16),
                pltpu.SemaphoreType.DMA(()),
            ],
            4 << 30,
        )(ride, *around, list_fine.T, transfer_ops, *earlier)

    def swap(x, axis, mask):
        return lax.ppermute(x, axis, [(i, i ^ mask) for i in range(lax.axis_size(axis))])

    work = {
        1: {"top": load, "a": lambda ride: fine(0, 0, [], ride)},
        2: {"a": lambda ride: fine(0, 1, done["a"], ride)},
        4: {"b": lambda ride: fine(1, 0, [], ride)},
        5: {"b": lambda ride: fine(1, 1, done["b"], ride)},
        6: {"mid": functools.partial(small, mid_kernel, list_mid.T)},
        7: {"low": functools.partial(small, low_kernel, list_low)},
    }
    done = {}
    total = top
    for step, mask in enumerate((1, 2, 6, 1, 2, 6, 8, 24)):
        axis = "col" if step < 3 else "row"
        other = swap(total, axis, mask) if axis == "col" or mask < rows else None
        for name, kernel in work.get(step, {}).items():
            total, *done[name] = kernel(total)
        if axis == "col":
            total = total + other
        elif step < 7:
            total = total if other is None else jnp.concatenate([total, other], axis=0)
        if step == 2:
            total = total.astype(BF16)
    other = total if other is None else other
    (far,) = call(
        down_kernel,
        [VMEM] * 3 + [HBM] * 2 + [VMEM] * 3 + [HBM],
        [shape((2, SIZE, FINE), F32)],
        [
            pltpu.VMEM((2, SIZE, FINE), F32),
            pltpu.VMEM((2, 2, SIZE, REACH), F32),
            pltpu.VMEM((3, OCTANTS) + octant_ops, BF16),
            pltpu.VMEM(octant_ops, BF16),
            pltpu.VMEM((FINE, FINE), BF16),
            pltpu.SemaphoreType.DMA((10,)),
        ],
        8 << 30,
        place=HBM,
    )(
        total, other, list_top.T, in_hbm(done["a"][0]), in_hbm(done["b"][0]), *done["mid"], *done["low"],
        *done["top"],
        downward_ops,
    )
    return far


def solution(mesh):
    split = P(None, None, ("row", "col"))
    lists = P(("row", "col"), None)
    return jax.shard_map(
        body,
        mesh=mesh,
        in_specs=(split, P(), P(), P(), P(), lists, lists, lists, P()),
        out_specs=split,
        check_vma=False,
    )
```

```python
import functools

import jax
import jax.numpy as jnp
from jax import lax
from jax.experimental import pallas as pl
from jax.experimental.pallas import tpu as pltpu
from jax.sharding import PartitionSpec as P

SIZE = 152
HALF = 64
FINE = 512
REACH = 256
ENTRIES = 16
GROUP = 8
OCTANTS = 8
BF16 = jnp.bfloat16
F32 = jnp.float32


def mm(a, b):
    return jnp.dot(a, b, preferred_element_type=F32)


def iota(shape, dim):
    return lax.broadcasted_iota(jnp.int32, shape, dim)


def combine(by_real, by_imag):
    turned = pltpu.roll(by_imag, HALF, 1)
    return by_real + jnp.where(iota(turned.shape, 1) < HALF, -turned, turned)


def box_order(lane):
    return (lane & 7) * 8 + ((lane & 63) >> 3)


def regroup(first, second):
    low = iota(first.shape, 1) < HALF
    return (
        jnp.where(low, first, pltpu.roll(second, HALF, 1)),
        jnp.where(low, pltpu.roll(first, HALF, 1), second),
    )


def apply_each(ops, columns, count):
    by_real = jnp.zeros((SIZE, 128), F32)
    by_imag = jnp.zeros((SIZE, 128), F32)
    for c in range(count):
        one = columns(c)
        by_real += mm(ops[c, 0], one)
        by_imag += mm(ops[c, 1], one)
    return combine(by_real, by_imag)


def tile(array, index):
    return array[:, 128 * index : 128 * (index + 1)]


def pass_on(ride, ride_out):
    def step(i, carry):
        part = pl.ds(pl.multiple_of(i * 256, 256), 256)
        ride_out[:, part] = ride[:, part]
        return carry

    lax.fori_loop(0, 2, step, 0)


def fill_places(places, row_to_col):
    def step(i, carry):
        begin = pl.multiple_of(i * 256, 256)
        row = iota((256, FINE), 0) + begin
        col = iota((256, FINE), 1)
        places[pl.ds(begin, 256), :] = (row == row_to_col(col)).astype(BF16)
        return carry

    lax.fori_loop(0, 2, step, 0)


def up_kernel(
    check_hbm, equiv_hbm, ops_hbm, to_left, to_right, top, check, equiv, ops, own_op, by_octant, sems
):
    first = [
        pltpu.make_async_copy(equiv_hbm, equiv, sems.at[4]),
        pltpu.make_async_copy(check_hbm, check, sems.at[5]),
    ]
    copies = [
        pltpu.make_async_copy(ops_hbm.at[level], ops.at[level], sems.at[level])
        for level in range(3)
    ]
    copies.append(pltpu.make_async_copy(ops_hbm.at[3, lax.axis_index("col")], own_op, sems.at[3]))
    for copy in first + copies:
        copy.start()
    fill_places(by_octant, lambda col: box_order(col) * 8 + (col >> 6))
    for copy in first:
        copy.wait()
    field = jnp.concatenate([check[0], check[1]], axis=1)
    by_real = mm(equiv[0], field)
    by_imag = mm(equiv[1], field)
    real = by_real[:, :FINE] - by_imag[:, FINE:]
    imag = by_real[:, FINE:] + by_imag[:, :FINE]
    dense = jnp.concatenate([real, imag], axis=0).astype(BF16)
    to_left[:, :REACH] = dense[:, :REACH]
    to_right[:, :REACH] = dense[:, REACH:]
    ordered = mm(dense, by_octant[...])
    children = []
    for pair in range(OCTANTS // 2):
        children += regroup(tile(ordered[:SIZE], pair), tile(ordered[SIZE:], pair))
    children = [child.astype(BF16) for child in children]
    copies[0].wait()
    packed = [apply_each(ops.at[0], lambda c: children[c], OCTANTS).astype(BF16)]
    lane = iota((SIZE, 128), 1) & 63
    for level, octant, steps in ((1, lane >> 3, (32, 16, 8)), (2, lane, (4, 2, 1))):
        copies[level].wait()
        below = packed[level - 1]
        by_real = mm(ops[level, 0, 0], below)
        by_imag = mm(ops[level, 0, 1], below)
        for c in range(1, OCTANTS):
            by_real = jnp.where(octant == c, mm(ops[level, c, 0], below), by_real)
            by_imag = jnp.where(octant == c, mm(ops[level, c, 1], below), by_imag)
        dense = combine(by_real, by_imag)
        for step in steps:
            dense = dense + pltpu.roll(dense, 128 - step, 1)
        packed.append(jnp.where(lane < steps[-1], dense, 0.0).astype(BF16))
    both = jnp.concatenate([packed[0].astype(F32), packed[1].astype(F32)], axis=0).astype(BF16)
    to_left[:, REACH:] = both
    to_right[:, REACH:] = both
    copies[3].wait()
    part = combine(mm(own_op[0], packed[2]), mm(own_op[1], packed[2]))
    flat = jnp.transpose(jnp.concatenate([part, jnp.zeros((104, 128), F32)], axis=0))
    top[:, :256] = flat[0:1, :]
    top[:, 256:] = flat[HALF : HALF + 1, :]


def load_kernel(ride, transfer_hbm, ride_out, transfer, sem):
    copy = pltpu.make_async_copy(transfer_hbm.at[3], transfer, sem)
    copy.start()
    ride_out[...] = ride[...]
    copy.wait()


def device_position():
    return lax.axis_index("row") * lax.axis_size("col") + lax.axis_index("col")


def translate_packed(around, codes, targets, ops, copies):
    select = jnp.concatenate(
        [(codes == targets[k : k + 1, :]).astype(BF16) for k in range(ENTRIES)], axis=1
    )
    picked = mm(around, select).astype(BF16)
    by_real = jnp.zeros((SIZE, 128), F32)
    by_imag = jnp.zeros((SIZE, 128), F32)
    for k in range(ENTRIES):
        if k % GROUP == 0:
            copies[k // GROUP].wait()
        by_real += mm(ops[k, 0], tile(picked, k))
        by_imag += mm(ops[k, 1], tile(picked, k))
    return combine(by_real, by_imag)


def start_copies(ops_hbm, level, ops, sems):
    copies = []
    for group in range(ENTRIES // GROUP):
        part = pl.ds(group * GROUP, GROUP)
        copies.append(pltpu.make_async_copy(ops_hbm.at[level, part], ops.at[part], sems.at[group]))
        copies[group].start()
    return copies


def low_kernel(ride, from_left, from_right, own, low_list, ops_hbm, ride_out, out, ops, sems):
    copies = start_copies(ops_hbm, 2, ops, sems)
    pass_on(ride, ride_out)
    lows = [ref[:, REACH:].astype(F32)[SIZE:] for ref in (own, from_left, from_right)]
    around = (lows[0] + pltpu.roll(lows[1], 8, 1) + pltpu.roll(lows[2], 16, 1)).astype(BF16)
    row = iota((128, 128), 0)
    lane = row & 63
    place = jnp.where(lane < 8, lane, jnp.where(lane < 16, lane - 16, lane - 8))
    codes = jnp.where(lane < 24, (row >> 6) * 1024 + place, -(1 << 20)).astype(F32)
    index = (low_list[...] - device_position() * 8).astype(F32)
    listed = jnp.transpose(jnp.concatenate([index, jnp.zeros((8, 112), F32)], axis=1))[:ENTRIES]
    listed = jnp.concatenate([listed, jnp.zeros((ENTRIES, 120), F32)], axis=1).astype(BF16)
    lane = iota((128, 128), 1)
    targets = mm(listed, (iota((128, 128), 0) == (lane & 63) >> 3).astype(BF16))
    targets = targets + jnp.where(iota(targets.shape, 1) < HALF, 0.0, 1024.0)
    out[...] = translate_packed(around, codes, targets, ops, copies)


def mid_kernel(ride, from_left, from_right, own, mid_t, ops_hbm, ride_out, out, ops, sems):
    copies = start_copies(ops_hbm, 1, ops, sems)
    pass_on(ride, ride_out)
    mids = [ref[:, REACH:].astype(F32)[:SIZE] for ref in (from_left, own, from_right)]
    around = jnp.concatenate(mids, axis=1).astype(BF16)
    row = iota((384, 128), 0)
    codes = ((row >> 6) & 1) * 1024 + box_order(row) + ((row >> 7) - 1) * HALF
    index = mid_t[...] - device_position() * HALF
    targets = jnp.concatenate([index, index + 1024], axis=1)
    out[...] = translate_packed(around, codes, targets, ops, copies)


def fine_kernel(part, ride, before, first, second, fine_t, ops_hbm, *refs):
    half, group = part
    earlier, (ride_out, out, window, picked, ops, sem) = refs[:-6], refs[-6:]
    begin = group * GROUP
    copy = pltpu.make_async_copy(ops_hbm.at[0, pl.ds(begin, GROUP)], ops, sem)
    copy.start()
    pass_on(ride, ride_out)
    window[:, :REACH] = before[:, :REACH]
    window[:, REACH : 2 * REACH] = first[:, :REACH]
    window[:, 2 * REACH :] = second[:, :REACH]
    index = fine_t[begin : begin + GROUP, half * REACH : (half + 1) * REACH]
    index = index - (device_position() * FINE + (half - 1) * REACH)
    row = iota((3 * REACH, REACH), 0)
    for k in range(GROUP):
        select = (row == index[k : k + 1, :]).astype(BF16)
        both = mm(window[...], select)
        picked[k, :, :REACH] = both[:SIZE].astype(BF16)
        picked[k, :, REACH:] = both[SIZE:].astype(BF16)
    copy.wait()
    by_real = jnp.zeros((SIZE, FINE), F32)
    by_imag = jnp.zeros((SIZE, FINE), F32)
    for k in range(GROUP):
        by_real += mm(ops[k, 0], picked[k])
        by_imag += mm(ops[k, 1], picked[k])
    real = by_real[:, :REACH] - by_imag[:, REACH:]
    imag = by_real[:, REACH:] + by_imag[:, :REACH]
    if earlier:
        real += earlier[0][0]
        imag += earlier[0][1]
    out[0] = real
    out[1] = imag


def down_kernel(
    tops, others, top_list, fine_a_hbm, fine_b, mid_near, low_near, transfer, down_hbm,
    out_hbm, out, fine_a, down, own_op, rows, sems,
):
    copies = [
        pltpu.make_async_copy(down_hbm.at[level], down.at[level], sems.at[level])
        for level in range(3)
    ]
    copies.append(pltpu.make_async_copy(down_hbm.at[3, lax.axis_index("col")], own_op, sems.at[3]))
    copies.append(pltpu.make_async_copy(fine_a_hbm, fine_a, sems.at[4]))
    for level in (3, 2, 1, 0, 4):
        copies[level].start()

    def fill(part, carry):
        begin = pl.multiple_of(part * HALF, HALF)
        lanes = pl.ds(pl.multiple_of(part * 256, 256), 256)
        held = [tops[:, lanes].astype(F32), others[:, lanes].astype(F32)]
        gap = jnp.zeros((HALF - 2 * tops.shape[0], 256), F32)
        rows[pl.ds(begin, HALF), :] = jnp.concatenate(held + [gap], axis=0)
        return carry

    lax.fori_loop(0, 2, fill, 0)
    dense = jnp.transpose(rows[...])[:SIZE].astype(BF16)
    own_row = lax.axis_index("row")
    place = top_list[...] ^ own_row
    place = place ^ ((place >> 1) & 0b01010)
    mine = iota(place.shape, 1) == own_row
    listed = jnp.sum(jnp.where(mine, place.astype(F32), 0.0), axis=1, keepdims=True)
    codes = (iota((128, 128), 0) - (iota((128, 128), 1) & HALF)).astype(F32)
    select = jnp.concatenate([(codes == listed[k : k + 1, :]).astype(BF16) for k in range(ENTRIES)], axis=1)
    picked = mm(dense, select).astype(BF16)
    local = apply_each(transfer, lambda k: tile(picked, k), ENTRIES).astype(BF16)
    copies[3].wait()
    local = combine(mm(own_op[0], local), mm(own_op[1], local)).astype(BF16)
    lane = iota((SIZE, 128), 1) & 63
    for level, at_level, octant in ((2, low_near, lane >> 3), (1, mid_near, lane & 7)):
        copies[level].wait()
        by_real = mm(down[level, 0, 0], local)
        by_imag = mm(down[level, 0, 1], local)
        for c in range(1, OCTANTS):
            by_real = jnp.where(octant == c, mm(down[level, c, 0], local), by_real)
            by_imag = jnp.where(octant == c, mm(down[level, c, 1], local), by_imag)
        local = (combine(by_real, by_imag) + at_level[...]).astype(BF16)
    copies[0].wait()
    real, imag = [], []
    for pair in range(OCTANTS // 2):
        terms = [
            combine(mm(down[0, c, 0], local), mm(down[0, c, 1], local))
            for c in (2 * pair, 2 * pair + 1)
        ]
        one_real, one_imag = regroup(*terms)
        real.append(one_real)
        imag.append(one_imag)
    copies[4].wait()
    row = iota((FINE, FINE), 0)
    col = iota((FINE, FINE), 1)
    places = (row == (col & 7) * HALF + (col >> 3)).astype(BF16)
    out_copies = []
    for part, terms in enumerate((real, imag)):
        term = jnp.concatenate(terms, axis=1)
        high = term.astype(BF16)
        low = (term - high.astype(F32)).astype(BF16)
        for half in range(2):
            columns = pl.ds(half * REACH, REACH)
            place = places[:, half * REACH : (half + 1) * REACH]
            near = fine_b if half else fine_a
            out[part, :, columns] = near[part] + mm(high, place) + mm(low, place)
            copy = pltpu.make_async_copy(
                out.at[part, :, columns], out_hbm.at[part, :, columns], sems.at[6 + 2 * part + half]
            )
            copy.start()
            out_copies.append(copy)
    for copy in out_copies:
        copy.wait()


def shape(dims, dtype):
    return jax.ShapeDtypeStruct(dims, dtype)


VMEM = pl.BlockSpec(memory_space=pltpu.VMEM)
SMEM = pl.BlockSpec(memory_space=pltpu.SMEM)
HBM = pl.BlockSpec(memory_space=pltpu.HBM)
INTERPRET = False


def in_hbm(x):
    return x if INTERPRET else pltpu.with_memory_space_constraint(x, pltpu.HBM)


def on_chip(dims, dtype):
    return shape(dims, dtype) if INTERPRET else pltpu.VMEM(dims, dtype)


def off_chip(dims, dtype):
    return shape(dims, dtype) if INTERPRET else pltpu.HBM(dims, dtype)


def call(kernel, ins, outs, scratch, flops, limit=16, place=VMEM):
    return pl.pallas_call(
        kernel,
        in_specs=ins,
        out_specs=[place] * len(outs),
        out_shape=outs,
        scratch_shapes=scratch,
        compiler_params=pltpu.CompilerParams(vmem_limit_bytes=limit << 20),
        cost_estimate=pl.CostEstimate(flops=flops, bytes_accessed=8 << 20, transcendentals=0),
        interpret=INTERPRET,
    )


def body(
    check_field, to_equiv, upward_ops, downward_ops, transfer_ops, list_fine, list_mid, list_low, list_top
):
    axes = ("row", "col")
    rows, cols = lax.axis_size("row"), lax.axis_size("col")
    count = rows * cols
    check_field, to_equiv, upward_ops, downward_ops, transfer_ops = [
        in_hbm(x) for x in (check_field, to_equiv, upward_ops, downward_ops, transfer_ops)
    ]
    octant_ops = (2, SIZE, SIZE)
    to_left, to_right, top = call(
        up_kernel,
        [HBM, HBM, HBM],
        [shape((2 * SIZE, 384), BF16), shape((2 * SIZE, 384), BF16), shape((1, 512), F32)],
        [
            pltpu.VMEM((2, SIZE, FINE), BF16),
            pltpu.VMEM(octant_ops, BF16),
            pltpu.VMEM((3, OCTANTS) + octant_ops, BF16),
            pltpu.VMEM(octant_ops, BF16),
            pltpu.VMEM((FINE, FINE), BF16),
            pltpu.SemaphoreType.DMA((6,)),
        ],
        4 << 30,
    )(check_field, to_equiv, upward_ops)
    from_left = lax.ppermute(to_right, axes, [(i, (i + 1) % count) for i in range(count)])
    from_right = lax.ppermute(to_left, axes, [(i, (i - 1) % count) for i in range(count)])

    def load(ride):
        return call(
            load_kernel,
            [VMEM, HBM],
            [shape(ride.shape, ride.dtype), on_chip((ENTRIES,) + octant_ops, BF16)],
            [pltpu.SemaphoreType.DMA(())],
            8 << 30,
        )(ride, transfer_ops)

    def small(kernel, listed, ride):
        return call(
            kernel,
            [VMEM] * 5 + [HBM],
            [shape(ride.shape, ride.dtype), shape((SIZE, 128), F32)],
            [pltpu.VMEM((ENTRIES,) + octant_ops, BF16), pltpu.SemaphoreType.DMA((2,))],
            3 << 30,
        )(ride, from_left, from_right, to_left, listed, transfer_ops)

    def fine(half, group, earlier, ride):
        around = (from_left, to_left, to_right) if half == 0 else (to_left, to_right, from_right)
        return call(
            functools.partial(fine_kernel, (half, group)),
            [VMEM] * 5 + [HBM] + [VMEM] * len(earlier),
            [shape(ride.shape, ride.dtype), (off_chip, on_chip)[half]((2, SIZE, REACH), F32) if group else shape((2, SIZE, REACH), F32)],
            [
                pltpu.VMEM((2 * SIZE, 3 * REACH), BF16),
                pltpu.VMEM((GROUP, SIZE, FINE), BF16),
                pltpu.VMEM((GROUP,) + octant_ops, BF16),
                pltpu.SemaphoreType.DMA(()),
            ],
            4 << 30,
        )(ride, *around, list_fine.T, transfer_ops, *earlier)

    def swap(x, axis, mask):
        return lax.ppermute(x, axis, [(i, i ^ mask) for i in range(lax.axis_size(axis))])

    work = {
        1: {"top": load, "a": lambda ride: fine(0, 0, [], ride)},
        2: {"a": lambda ride: fine(0, 1, done["a"], ride)},
        4: {"mid": functools.partial(small, mid_kernel, list_mid.T)},
        5: {"low": functools.partial(small, low_kernel, list_low)},
        6: {"b": lambda ride: fine(1, 0, [], ride)},
        7: {"b": lambda ride: fine(1, 1, done["b"], ride)},
    }
    done = {}
    total = top
    for step, mask in enumerate((1, 2, 6, 1, 2, 6, 8, 24)):
        axis = "col" if step < 3 else "row"
        other = swap(total, axis, mask) if axis == "col" or mask < rows else None
        for name, kernel in work.get(step, {}).items():
            total, *done[name] = kernel(total)
        if axis == "col":
            total = total + other
        elif step < 7:
            total = total if other is None else jnp.concatenate([total, other], axis=0)
        if step == 2:
            total = total.astype(BF16)
    other = total if other is None else other
    (far,) = call(
        down_kernel,
        [VMEM] * 3 + [HBM] + [VMEM] * 4 + [HBM],
        [shape((2, SIZE, FINE), F32)],
        [
            pltpu.VMEM((2, SIZE, FINE), F32),
            pltpu.VMEM((2, SIZE, REACH), F32),
            pltpu.VMEM((3, OCTANTS) + octant_ops, BF16),
            pltpu.VMEM(octant_ops, BF16),
            pltpu.VMEM((128, 256), F32),
            pltpu.SemaphoreType.DMA((10,)),
        ],
        8 << 30,
        place=HBM,
    )(
        total, other, list_top.T, in_hbm(done["a"][0]), *done["b"], *done["mid"], *done["low"],
        *done["top"],
        downward_ops,
    )
    return far


def solution(mesh):
    split = P(None, None, ("row", "col"))
    lists = P(("row", "col"), None)
    return jax.shard_map(
        body,
        mesh=mesh,
        in_specs=(split, P(), P(), P(), P(), lists, lists, lists, P()),
        out_specs=split,
        check_vma=False,
    )
```

```python
import functools

import jax
import jax.numpy as jnp
from jax import lax
from jax.experimental import pallas as pl
from jax.experimental.pallas import tpu as pltpu
from jax.sharding import PartitionSpec as P

SIZE = 152
HALF = 64
FINE = 512
REACH = 256
ENTRIES = 16
GROUP = 8
OCTANTS = 8
BF16 = jnp.bfloat16
F32 = jnp.float32


def mm(a, b):
    return jnp.dot(a, b, preferred_element_type=F32)


def iota(shape, dim):
    return lax.broadcasted_iota(jnp.int32, shape, dim)


def combine(by_real, by_imag):
    turned = pltpu.roll(by_imag, HALF, 1)
    return by_real + jnp.where(iota(turned.shape, 1) < HALF, -turned, turned)


def box_order(lane):
    return ((lane & 3) + ((lane & 32) >> 3)) * 8 + ((lane >> 2) & 7)


def unpack(halo):
    rows = halo[2 * SIZE :, :].astype(F32)
    return jnp.concatenate([rows[:, :128], rows[8:, 128:]], axis=0)


def regroup(first, second):
    low = iota(first.shape, 1) < HALF
    return (
        jnp.where(low, first, pltpu.roll(second, HALF, 1)),
        jnp.where(low, pltpu.roll(first, HALF, 1), second),
    )


def apply_each(ops, columns, count):
    by_real = jnp.zeros((SIZE, 128), F32)
    by_imag = jnp.zeros((SIZE, 128), F32)
    for c in range(count):
        one = columns(c)
        by_real += mm(ops[c, 0], one)
        by_imag += mm(ops[c, 1], one)
    return combine(by_real, by_imag)


def tile(array, index):
    return array[:, 128 * index : 128 * (index + 1)]


def pass_on(ride, ride_out):
    def step(i, carry):
        part = pl.ds(pl.multiple_of(i * 256, 256), 256)
        ride_out[:, part] = ride[:, part]
        return carry

    lax.fori_loop(0, 2, step, 0)


def fill_places(places, row_to_col):
    def step(i, carry):
        begin = pl.multiple_of(i * 256, 256)
        row = iota((256, FINE), 0) + begin
        col = iota((256, FINE), 1)
        places[pl.ds(begin, 256), :] = (row == row_to_col(col)).astype(BF16)
        return carry

    lax.fori_loop(0, 2, step, 0)


def up_kernel(
    check_hbm, equiv_hbm, ops_hbm, to_left, to_right, small_out, top, check, equiv, ops, own_op, by_octant, sems
):
    first = [
        pltpu.make_async_copy(equiv_hbm, equiv, sems.at[4]),
        pltpu.make_async_copy(check_hbm, check, sems.at[5]),
    ]
    copies = [
        pltpu.make_async_copy(ops_hbm.at[level], ops.at[level], sems.at[level])
        for level in range(3)
    ]
    copies.append(pltpu.make_async_copy(ops_hbm.at[3, lax.axis_index("col")], own_op, sems.at[3]))
    for copy in first + copies:
        copy.start()
    fill_places(by_octant, lambda col: box_order(col) * 8 + (col >> 6))
    for copy in first:
        copy.wait()
    field = jnp.concatenate([check[0], check[1]], axis=1)
    by_real = mm(equiv[0], field)
    by_imag = mm(equiv[1], field)
    real = by_real[:, :FINE] - by_imag[:, FINE:]
    imag = by_real[:, FINE:] + by_imag[:, :FINE]
    dense = jnp.concatenate([real, imag], axis=0).astype(BF16)
    to_left[: 2 * SIZE, :] = dense[:, :REACH]
    to_right[: 2 * SIZE, :] = dense[:, REACH:]
    ordered = mm(dense, by_octant[...])
    children = []
    for pair in range(OCTANTS // 2):
        children += regroup(tile(ordered[:SIZE], pair), tile(ordered[SIZE:], pair))
    children = [child.astype(BF16) for child in children]
    copies[0].wait()
    packed = [apply_each(ops.at[0], lambda c: children[c], OCTANTS).astype(BF16)]
    lane = iota((SIZE, 128), 1) & 63
    places = ((lane >> 2) & 7, (16, 8, 4), (lane & 31) < 4), ((lane & 3) + (lane >> 5) * 4, (32, 2, 1), lane == 0)
    for level, (octant, steps, held) in enumerate(places, 1):
        copies[level].wait()
        below = packed[level - 1]
        by_real = mm(ops[level, 0, 0], below)
        by_imag = mm(ops[level, 0, 1], below)
        for c in range(1, OCTANTS):
            by_real = jnp.where(octant == c, mm(ops[level, c, 0], below), by_real)
            by_imag = jnp.where(octant == c, mm(ops[level, c, 1], below), by_imag)
        dense = combine(by_real, by_imag)
        for step in steps:
            dense = dense + pltpu.roll(dense, 128 - step, 1)
        packed.append(jnp.where(held, dense, 0.0).astype(BF16))
    mid, low = packed[0].astype(F32), packed[1].astype(F32)
    small_out[...] = jnp.concatenate([mid, low], axis=0).astype(BF16)
    to_neighbour = (
        (to_left, jnp.where(lane < 32, mid, pltpu.roll(low, 32, 1))),
        (to_right, jnp.where(lane < 32, pltpu.roll(low, 96, 1), mid)),
    )
    for halo, columns in to_neighbour:
        halo[2 * SIZE :, :] = jnp.concatenate([columns[:80], columns[72:]], axis=1).astype(BF16)
    copies[3].wait()
    part = combine(mm(own_op[0], packed[2]), mm(own_op[1], packed[2]))
    flat = jnp.transpose(jnp.concatenate([part, jnp.zeros((104, 128), F32)], axis=0))
    top[:, :256] = flat[0:1, :]
    top[:, 256:] = flat[HALF : HALF + 1, :]


def load_kernel(ride, transfer_hbm, ride_out, transfer, sem):
    copy = pltpu.make_async_copy(transfer_hbm.at[3], transfer, sem)
    copy.start()
    ride_out[...] = ride[...]
    copy.wait()


def device_position():
    return lax.axis_index("row") * lax.axis_size("col") + lax.axis_index("col")


def translate_packed(around, codes, targets, ops, copies):
    select = jnp.concatenate(
        [(codes == targets[k : k + 1, :]).astype(BF16) for k in range(ENTRIES)], axis=1
    )
    picked = mm(around, select).astype(BF16)
    by_real = jnp.zeros((SIZE, 128), F32)
    by_imag = jnp.zeros((SIZE, 128), F32)
    for k in range(ENTRIES):
        if k % GROUP == 0:
            copies[k // GROUP].wait()
        by_real += mm(ops[k, 0], tile(picked, k))
        by_imag += mm(ops[k, 1], tile(picked, k))
    return combine(by_real, by_imag)


def start_copies(ops_hbm, level, ops, sems):
    copies = []
    for group in range(ENTRIES // GROUP):
        part = pl.ds(group * GROUP, GROUP)
        copies.append(pltpu.make_async_copy(ops_hbm.at[level, part], ops.at[part], sems.at[group]))
        copies[group].start()
    return copies


def low_kernel(ride, from_left, from_right, own, low_list, ops_hbm, ride_out, out, ops, sems):
    copies = start_copies(ops_hbm, 2, ops, sems)
    pass_on(ride, ride_out)
    lane = iota((SIZE, 128), 1) & 63
    left = jnp.where(lane < 4, unpack(from_left), 0.0)
    right = jnp.where((lane >= 32) & (lane < 36), unpack(from_right), 0.0)
    around = (own[...].astype(F32)[SIZE:] + pltpu.roll(left, 8, 1) + pltpu.roll(right, 8, 1)).astype(BF16)
    row = iota((128, 128), 0)
    first = (row & 31) < 4
    place = (row & 3) + jnp.where((row & 32) == 0, jnp.where(first, 0, -4), jnp.where(first, 4, 8))
    held = first | ((row & 31) >> 2 == 2)
    codes = jnp.where(held, (row >> 6) * 1024 + place, -(1 << 20)).astype(F32)
    index = (low_list[...] - device_position() * 8).astype(F32)
    listed = jnp.transpose(jnp.concatenate([index, jnp.zeros((8, 112), F32)], axis=1))[:ENTRIES]
    listed = jnp.concatenate([listed, jnp.zeros((ENTRIES, 120), F32)], axis=1).astype(BF16)
    lane = iota((128, 128), 1)
    targets = mm(listed, (iota((128, 128), 0) == (lane & 63) >> 3).astype(BF16))
    targets = targets + jnp.where(iota(targets.shape, 1) < HALF, 0.0, 1024.0)
    out[...] = translate_packed(around, codes, targets, ops, copies)


def mid_kernel(ride, from_left, from_right, own, mid_t, ops_hbm, ride_out, out, ops, sems):
    copies = start_copies(ops_hbm, 1, ops, sems)
    pass_on(ride, ride_out)
    mids = [unpack(from_left), own[...].astype(F32)[:SIZE], unpack(from_right)]
    around = jnp.concatenate(mids, axis=1).astype(BF16)
    row = iota((384, 128), 0)
    device = (row >> 7) - 1
    held = (device == 0) | ((row & 32 == 32) & (device < 0)) | ((row & 32 == 0) & (device > 0))
    codes = jnp.where(held, ((row >> 6) & 1) * 1024 + box_order(row) + device * HALF, -(1 << 20))
    index = mid_t[...] - device_position() * HALF
    targets = jnp.concatenate([index, index + 1024], axis=1)
    out[...] = translate_packed(around, codes, targets, ops, copies)


def fine_kernel(part, ride, before, first, second, fine_t, ops_hbm, *refs):
    half, group = part
    earlier, (ride_out, out, window, picked, ops, sem) = refs[:-6], refs[-6:]
    begin = group * GROUP
    copy = pltpu.make_async_copy(ops_hbm.at[0, pl.ds(begin, GROUP)], ops, sem)
    copy.start()
    pass_on(ride, ride_out)
    for j, halo in enumerate((before, first, second)):
        window[:, REACH * j : REACH * (j + 1)] = halo[: 2 * SIZE, :]
    index = fine_t[begin : begin + GROUP, half * REACH : (half + 1) * REACH]
    index = index - (device_position() * FINE + (half - 1) * REACH)
    row = iota((3 * REACH, REACH), 0)
    for k in range(GROUP):
        select = (row == index[k : k + 1, :]).astype(BF16)
        both = mm(window[...], select)
        picked[k, :, :REACH] = both[:SIZE].astype(BF16)
        picked[k, :, REACH:] = both[SIZE:].astype(BF16)
    copy.wait()
    by_real = jnp.zeros((SIZE, FINE), F32)
    by_imag = jnp.zeros((SIZE, FINE), F32)
    for k in range(GROUP):
        by_real += mm(ops[k, 0], picked[k])
        by_imag += mm(ops[k, 1], picked[k])
    real = by_real[:, :REACH] - by_imag[:, REACH:]
    imag = by_real[:, REACH:] + by_imag[:, :REACH]
    if earlier:
        real += earlier[0][0]
        imag += earlier[0][1]
    out[0] = real
    out[1] = imag


def down_kernel(
    tops, others, top_list, fine_a_hbm, fine_b, mid_near, low_near, transfer, down_hbm,
    out_hbm, out, fine_a, down, own_op, rows, sems,
):
    copies = [
        pltpu.make_async_copy(down_hbm.at[level], down.at[level], sems.at[level])
        for level in range(3)
    ]
    copies.append(pltpu.make_async_copy(down_hbm.at[3, lax.axis_index("col")], own_op, sems.at[3]))
    copies.append(pltpu.make_async_copy(fine_a_hbm, fine_a, sems.at[4]))
    for level in (3, 2, 1, 0, 4):
        copies[level].start()

    def fill(part, carry):
        begin = pl.multiple_of(part * HALF, HALF)
        lanes = pl.ds(pl.multiple_of(part * 256, 256), 256)
        held = [tops[:, lanes].astype(F32), others[:, lanes].astype(F32)]
        gap = jnp.zeros((HALF - 2 * tops.shape[0], 256), F32)
        rows[pl.ds(begin, HALF), :] = jnp.concatenate(held + [gap], axis=0)
        return carry

    lax.fori_loop(0, 2, fill, 0)
    dense = jnp.transpose(rows[...])[:SIZE].astype(BF16)
    own_row = lax.axis_index("row")
    place = top_list[...] ^ own_row
    place = place ^ ((place >> 1) & 0b01010)
    mine = iota(place.shape, 1) == own_row
    listed = jnp.sum(jnp.where(mine, place.astype(F32), 0.0), axis=1, keepdims=True)
    codes = (iota((128, 128), 0) - (iota((128, 128), 1) & HALF)).astype(F32)
    select = jnp.concatenate([(codes == listed[k : k + 1, :]).astype(BF16) for k in range(ENTRIES)], axis=1)
    picked = mm(dense, select).astype(BF16)
    local = apply_each(transfer, lambda k: tile(picked, k), ENTRIES).astype(BF16)
    copies[3].wait()
    local = combine(mm(own_op[0], local), mm(own_op[1], local)).astype(BF16)
    lane = iota((SIZE, 128), 1) & 63
    for level, at_level, octant in ((2, low_near, lane >> 3), (1, mid_near, lane & 7)):
        copies[level].wait()
        by_real = mm(down[level, 0, 0], local)
        by_imag = mm(down[level, 0, 1], local)
        for c in range(1, OCTANTS):
            by_real = jnp.where(octant == c, mm(down[level, c, 0], local), by_real)
            by_imag = jnp.where(octant == c, mm(down[level, c, 1], local), by_imag)
        local = (combine(by_real, by_imag) + at_level[...]).astype(BF16)
    copies[0].wait()
    real, imag = [], []
    for pair in range(OCTANTS // 2):
        terms = [
            combine(mm(down[0, c, 0], local), mm(down[0, c, 1], local))
            for c in (2 * pair, 2 * pair + 1)
        ]
        one_real, one_imag = regroup(*terms)
        real.append(one_real)
        imag.append(one_imag)
    copies[4].wait()
    row = iota((FINE, FINE), 0)
    col = iota((FINE, FINE), 1)
    places = (row == (col & 7) * HALF + (col >> 3)).astype(BF16)
    out_copies = []
    for part, terms in enumerate((real, imag)):
        term = jnp.concatenate(terms, axis=1)
        high = term.astype(BF16)
        low = (term - high.astype(F32)).astype(BF16)
        for half in range(2):
            columns = pl.ds(half * REACH, REACH)
            place = places[:, half * REACH : (half + 1) * REACH]
            near = fine_b if half else fine_a
            out[part, :, columns] = near[part] + mm(high, place) + mm(low, place)
            copy = pltpu.make_async_copy(
                out.at[part, :, columns], out_hbm.at[part, :, columns], sems.at[6 + 2 * part + half]
            )
            copy.start()
            out_copies.append(copy)
    for copy in out_copies:
        copy.wait()


def shape(dims, dtype):
    return jax.ShapeDtypeStruct(dims, dtype)


VMEM = pl.BlockSpec(memory_space=pltpu.VMEM)
SMEM = pl.BlockSpec(memory_space=pltpu.SMEM)
HBM = pl.BlockSpec(memory_space=pltpu.HBM)
INTERPRET = False


def in_hbm(x):
    return x if INTERPRET else pltpu.with_memory_space_constraint(x, pltpu.HBM)


def on_chip(dims, dtype):
    return shape(dims, dtype) if INTERPRET else pltpu.VMEM(dims, dtype)


def off_chip(dims, dtype):
    return shape(dims, dtype) if INTERPRET else pltpu.HBM(dims, dtype)


def call(kernel, ins, outs, scratch, flops, limit=16, place=VMEM):
    return pl.pallas_call(
        kernel,
        in_specs=ins,
        out_specs=[place] * len(outs),
        out_shape=outs,
        scratch_shapes=scratch,
        compiler_params=pltpu.CompilerParams(vmem_limit_bytes=limit << 20),
        cost_estimate=pl.CostEstimate(flops=flops, bytes_accessed=8 << 20, transcendentals=0),
        interpret=INTERPRET,
    )


def body(
    check_field, to_equiv, upward_ops, downward_ops, transfer_ops, list_fine, list_mid, list_low, list_top
):
    axes = ("row", "col")
    rows, cols = lax.axis_size("row"), lax.axis_size("col")
    count = rows * cols
    check_field, to_equiv, upward_ops, downward_ops, transfer_ops = [
        in_hbm(x) for x in (check_field, to_equiv, upward_ops, downward_ops, transfer_ops)
    ]
    octant_ops = (2, SIZE, SIZE)
    to_left, to_right, own_small, top = call(
        up_kernel,
        [HBM, HBM, HBM],
        [
            shape((2 * SIZE + 80, REACH), BF16),
            shape((2 * SIZE + 80, REACH), BF16),
            shape((2 * SIZE, 128), BF16),
            shape((1, 512), F32),
        ],
        [
            pltpu.VMEM((2, SIZE, FINE), BF16),
            pltpu.VMEM(octant_ops, BF16),
            pltpu.VMEM((3, OCTANTS) + octant_ops, BF16),
            pltpu.VMEM(octant_ops, BF16),
            pltpu.VMEM((FINE, FINE), BF16),
            pltpu.SemaphoreType.DMA((6,)),
        ],
        4 << 30,
    )(check_field, to_equiv, upward_ops)
    from_left = lax.ppermute(to_right, axes, [(i, (i + 1) % count) for i in range(count)])
    from_right = lax.ppermute(to_left, axes, [(i, (i - 1) % count) for i in range(count)])

    def load(ride):
        return call(
            load_kernel,
            [VMEM, HBM],
            [shape(ride.shape, ride.dtype), on_chip((ENTRIES,) + octant_ops, BF16)],
            [pltpu.SemaphoreType.DMA(())],
            8 << 30,
        )(ride, transfer_ops)

    def small(kernel, listed, ride):
        return call(
            kernel,
            [VMEM] * 5 + [HBM],
            [shape(ride.shape, ride.dtype), shape((SIZE, 128), F32)],
            [pltpu.VMEM((ENTRIES,) + octant_ops, BF16), pltpu.SemaphoreType.DMA((2,))],
            3 << 30,
        )(ride, from_left, from_right, own_small, listed, transfer_ops)

    def fine(half, group, earlier, ride):
        around = (from_left, to_left, to_right) if half == 0 else (to_left, to_right, from_right)
        return call(
            functools.partial(fine_kernel, (half, group)),
            [VMEM] * 5 + [HBM] + [VMEM] * len(earlier),
            [shape(ride.shape, ride.dtype), (off_chip, on_chip)[half]((2, SIZE, REACH), F32) if group else shape((2, SIZE, REACH), F32)],
            [
                pltpu.VMEM((2 * SIZE, 3 * REACH), BF16),
                pltpu.VMEM((GROUP, SIZE, FINE), BF16),
                pltpu.VMEM((GROUP,) + octant_ops, BF16),
                pltpu.SemaphoreType.DMA(()),
            ],
            4 << 30,
        )(ride, *around, list_fine.T, transfer_ops, *earlier)

    def swap(x, axis, mask):
        return lax.ppermute(x, axis, [(i, i ^ mask) for i in range(lax.axis_size(axis))])

    work = {
        1: {"top": load, "a": lambda ride: fine(0, 0, [], ride)},
        2: {"a": lambda ride: fine(0, 1, done["a"], ride)},
        4: {"mid": functools.partial(small, mid_kernel, list_mid.T)},
        5: {"low": functools.partial(small, low_kernel, list_low)},
        6: {"b": lambda ride: fine(1, 0, [], ride)},
        7: {"b": lambda ride: fine(1, 1, done["b"], ride)},
    }
    done = {}
    total = top
    for step, mask in enumerate((1, 2, 6, 1, 2, 6, 8, 24)):
        axis = "col" if step < 3 else "row"
        other = swap(total, axis, mask) if axis == "col" or mask < rows else None
        for name, kernel in work.get(step, {}).items():
            total, *done[name] = kernel(total)
        if axis == "col":
            total = total + other
        elif step < 7:
            total = total if other is None else jnp.concatenate([total, other], axis=0)
        if step == 2:
            total = total.astype(BF16)
    other = total if other is None else other
    (far,) = call(
        down_kernel,
        [VMEM] * 3 + [HBM] + [VMEM] * 4 + [HBM],
        [shape((2, SIZE, FINE), F32)],
        [
            pltpu.VMEM((2, SIZE, FINE), F32),
            pltpu.VMEM((2, SIZE, REACH), F32),
            pltpu.VMEM((3, OCTANTS) + octant_ops, BF16),
            pltpu.VMEM(octant_ops, BF16),
            pltpu.VMEM((128, 256), F32),
            pltpu.SemaphoreType.DMA((10,)),
        ],
        8 << 30,
        place=HBM,
    )(
        total, other, list_top.T, in_hbm(done["a"][0]), *done["b"], *done["mid"], *done["low"],
        *done["top"],
        downward_ops,
    )
    return far


def solution(mesh):
    split = P(None, None, ("row", "col"))
    lists = P(("row", "col"), None)
    return jax.shard_map(
        body,
        mesh=mesh,
        in_specs=(split, P(), P(), P(), P(), lists, lists, lists, P()),
        out_specs=split,
        check_vma=False,
    )
```

```python
import functools

import jax
import jax.numpy as jnp
from jax import lax
from jax.experimental import pallas as pl
from jax.experimental.pallas import tpu as pltpu
from jax.sharding import PartitionSpec as P

SIZE = 152
HALF = 64
FINE = 512
REACH = 256
ENTRIES = 16
GROUP = 8
OCTANTS = 8
BF16 = jnp.bfloat16
F32 = jnp.float32


def mm(a, b):
    return jnp.dot(a, b, preferred_element_type=F32)


def iota(shape, dim):
    return lax.broadcasted_iota(jnp.int32, shape, dim)


def combine(by_real, by_imag):
    turned = pltpu.roll(by_imag, HALF, 1)
    return by_real + jnp.where(iota(turned.shape, 1) < HALF, -turned, turned)


def box_order(lane):
    return ((lane & 3) + ((lane & 32) >> 3)) * 8 + ((lane >> 2) & 7)


def unpack(halo):
    rows = halo[2 * SIZE :, :].astype(F32)
    return jnp.concatenate([rows[:, :128], rows[8:, 128:]], axis=0)


def regroup(first, second):
    low = iota(first.shape, 1) < HALF
    return (
        jnp.where(low, first, pltpu.roll(second, HALF, 1)),
        jnp.where(low, pltpu.roll(first, HALF, 1), second),
    )


def apply_each(ops, columns, count):
    by_real = jnp.zeros((SIZE, 128), F32)
    by_imag = jnp.zeros((SIZE, 128), F32)
    for c in range(count):
        one = columns(c)
        by_real += mm(ops[c, 0], one)
        by_imag += mm(ops[c, 1], one)
    return combine(by_real, by_imag)


def tile(array, index):
    return array[:, 128 * index : 128 * (index + 1)]


def pass_on(ride, ride_out):
    def step(i, carry):
        part = pl.ds(pl.multiple_of(i * 256, 256), 256)
        ride_out[:, part] = ride[:, part]
        return carry

    lax.fori_loop(0, 2, step, 0)


def fill_places(places, row_to_col):
    def step(i, carry):
        begin = pl.multiple_of(i * 256, 256)
        row = iota((256, FINE), 0) + begin
        col = iota((256, FINE), 1)
        places[pl.ds(begin, 256), :] = (row == row_to_col(col)).astype(BF16)
        return carry

    lax.fori_loop(0, 2, step, 0)


def up_kernel(
    check_hbm, equiv_hbm, ops_hbm, to_left, to_right, small_out, top, check, equiv, ops, own_op, by_octant, sems
):
    first = [
        pltpu.make_async_copy(equiv_hbm, equiv, sems.at[4]),
        pltpu.make_async_copy(check_hbm, check, sems.at[5]),
    ]
    copies = [
        pltpu.make_async_copy(ops_hbm.at[level], ops.at[level], sems.at[level])
        for level in range(3)
    ]
    copies.append(pltpu.make_async_copy(ops_hbm.at[3, lax.axis_index("col")], own_op, sems.at[3]))
    for copy in first + copies:
        copy.start()
    fill_places(by_octant, lambda col: box_order(col) * 8 + (col >> 6))
    for copy in first:
        copy.wait()
    field = jnp.concatenate([check[0], check[1]], axis=1)
    by_real = mm(equiv[0], field)
    by_imag = mm(equiv[1], field)
    real = by_real[:, :FINE] - by_imag[:, FINE:]
    imag = by_real[:, FINE:] + by_imag[:, :FINE]
    dense = jnp.concatenate([real, imag], axis=0).astype(BF16)
    to_left[: 2 * SIZE, :] = dense[:, :REACH]
    to_right[: 2 * SIZE, :] = dense[:, REACH:]
    ordered = mm(dense, by_octant[...])
    children = []
    for pair in range(OCTANTS // 2):
        children += regroup(tile(ordered[:SIZE], pair), tile(ordered[SIZE:], pair))
    children = [child.astype(BF16) for child in children]
    copies[0].wait()
    packed = [apply_each(ops.at[0], lambda c: children[c], OCTANTS).astype(BF16)]
    lane = iota((SIZE, 128), 1) & 63
    places = ((lane >> 2) & 7, (16, 8, 4), (lane & 31) < 4), ((lane & 3) + (lane >> 5) * 4, (32, 2, 1), lane == 0)
    for level, (octant, steps, held) in enumerate(places, 1):
        copies[level].wait()
        below = packed[level - 1]
        by_real = mm(ops[level, 0, 0], below)
        by_imag = mm(ops[level, 0, 1], below)
        for c in range(1, OCTANTS):
            by_real = jnp.where(octant == c, mm(ops[level, c, 0], below), by_real)
            by_imag = jnp.where(octant == c, mm(ops[level, c, 1], below), by_imag)
        dense = combine(by_real, by_imag)
        for step in steps:
            dense = dense + pltpu.roll(dense, 128 - step, 1)
        packed.append(jnp.where(held, dense, 0.0).astype(BF16))
    mid, low = packed[0].astype(F32), packed[1].astype(F32)
    small_out[...] = jnp.concatenate([mid, low], axis=0).astype(BF16)
    to_neighbour = (
        (to_left, jnp.where(lane < 32, mid, pltpu.roll(low, 32, 1))),
        (to_right, jnp.where(lane < 32, pltpu.roll(low, 96, 1), mid)),
    )
    for halo, columns in to_neighbour:
        halo[2 * SIZE :, :] = jnp.concatenate([columns[:80], columns[72:]], axis=1).astype(BF16)
    copies[3].wait()
    part = combine(mm(own_op[0], packed[2]), mm(own_op[1], packed[2]))
    flat = jnp.transpose(jnp.concatenate([part, jnp.zeros((104, 128), F32)], axis=0))
    top[:, :256] = flat[0:1, :]
    top[:, 256:] = flat[HALF : HALF + 1, :]


def load_kernel(ride, transfer_hbm, ride_out, transfer, sem):
    copy = pltpu.make_async_copy(transfer_hbm.at[3], transfer, sem)
    copy.start()
    ride_out[...] = ride[...]
    copy.wait()


def device_position():
    return lax.axis_index("row") * lax.axis_size("col") + lax.axis_index("col")


def translate_packed(around, codes, targets, ops, copies):
    select = jnp.concatenate(
        [(codes == targets[k : k + 1, :]).astype(BF16) for k in range(ENTRIES)], axis=1
    )
    picked = mm(around, select).astype(BF16)
    by_real = jnp.zeros((SIZE, 128), F32)
    by_imag = jnp.zeros((SIZE, 128), F32)
    for k in range(ENTRIES):
        if k % GROUP == 0:
            copies[k // GROUP].wait()
        by_real += mm(ops[k, 0], tile(picked, k))
        by_imag += mm(ops[k, 1], tile(picked, k))
    return combine(by_real, by_imag)


def start_copies(ops_hbm, level, ops, sems):
    copies = []
    for group in range(ENTRIES // GROUP):
        part = pl.ds(group * GROUP, GROUP)
        copies.append(pltpu.make_async_copy(ops_hbm.at[level, part], ops.at[part], sems.at[group]))
        copies[group].start()
    return copies


def low_kernel(ride, from_left, from_right, own, low_list, ops_hbm, ride_out, out, ops, sems):
    copies = start_copies(ops_hbm, 2, ops, sems)
    pass_on(ride, ride_out)
    lane = iota((SIZE, 128), 1) & 63
    left = jnp.where(lane < 4, unpack(from_left), 0.0)
    right = jnp.where((lane >= 32) & (lane < 36), unpack(from_right), 0.0)
    around = (own[...].astype(F32)[SIZE:] + pltpu.roll(left, 8, 1) + pltpu.roll(right, 8, 1)).astype(BF16)
    row = iota((128, 128), 0)
    first = (row & 31) < 4
    place = (row & 3) + jnp.where((row & 32) == 0, jnp.where(first, 0, -4), jnp.where(first, 4, 8))
    held = first | ((row & 31) >> 2 == 2)
    codes = jnp.where(held, (row >> 6) * 1024 + place, -(1 << 20)).astype(F32)
    index = (low_list[...] - device_position() * 8).astype(F32)
    listed = jnp.transpose(jnp.concatenate([index, jnp.zeros((8, 112), F32)], axis=1))[:ENTRIES]
    listed = jnp.concatenate([listed, jnp.zeros((ENTRIES, 120), F32)], axis=1).astype(BF16)
    lane = iota((128, 128), 1)
    targets = mm(listed, (iota((128, 128), 0) == (lane & 63) >> 3).astype(BF16))
    targets = targets + jnp.where(iota(targets.shape, 1) < HALF, 0.0, 1024.0)
    out[...] = translate_packed(around, codes, targets, ops, copies)


def mid_kernel(ride, from_left, from_right, own, mid_t, ops_hbm, ride_out, out, ops, sems):
    copies = start_copies(ops_hbm, 1, ops, sems)
    pass_on(ride, ride_out)
    mids = [unpack(from_left), own[...].astype(F32)[:SIZE], unpack(from_right)]
    around = jnp.concatenate(mids, axis=1).astype(BF16)
    row = iota((384, 128), 0)
    device = (row >> 7) - 1
    held = (device == 0) | ((row & 32 == 32) & (device < 0)) | ((row & 32 == 0) & (device > 0))
    codes = jnp.where(held, ((row >> 6) & 1) * 1024 + box_order(row) + device * HALF, -(1 << 20))
    index = mid_t[...] - device_position() * HALF
    targets = jnp.concatenate([index, index + 1024], axis=1)
    out[...] = translate_packed(around, codes, targets, ops, copies)


def fine_kernel(part, ride, before, first, second, fine_t, ops_hbm, *refs):
    half, begin, size = part
    earlier, (ride_out, out, window, picked, ops, sem) = refs[:-6], refs[-6:]
    copy = pltpu.make_async_copy(ops_hbm.at[0, pl.ds(begin, size)], ops, sem)
    copy.start()
    pass_on(ride, ride_out)
    for j, halo in enumerate((before, first, second)):
        window[:, REACH * j : REACH * (j + 1)] = halo[: 2 * SIZE, :]
    index = fine_t[begin : begin + size, half * REACH : (half + 1) * REACH]
    index = index - (device_position() * FINE + (half - 1) * REACH)
    row = iota((3 * REACH, REACH), 0)
    for k in range(size):
        select = (row == index[k : k + 1, :]).astype(BF16)
        both = mm(window[...], select)
        picked[k, :, :REACH] = both[:SIZE].astype(BF16)
        picked[k, :, REACH:] = both[SIZE:].astype(BF16)
    copy.wait()
    by_real = jnp.zeros((SIZE, FINE), F32)
    by_imag = jnp.zeros((SIZE, FINE), F32)
    for k in range(size):
        by_real += mm(ops[k, 0], picked[k])
        by_imag += mm(ops[k, 1], picked[k])
    real = by_real[:, :REACH] - by_imag[:, REACH:]
    imag = by_real[:, REACH:] + by_imag[:, :REACH]
    if earlier:
        real += earlier[0][0]
        imag += earlier[0][1]
    out[0] = real
    out[1] = imag


def down_kernel(
    tops, others, top_list, fine_a_hbm, fine_b, mid_near, low_near, transfer, down_hbm,
    out_hbm, out, fine_a, down, own_op, rows, sems,
):
    copies = [
        pltpu.make_async_copy(down_hbm.at[level], down.at[level], sems.at[level])
        for level in range(3)
    ]
    copies.append(pltpu.make_async_copy(down_hbm.at[3, lax.axis_index("col")], own_op, sems.at[3]))
    copies.append(pltpu.make_async_copy(fine_a_hbm, fine_a, sems.at[4]))
    for level in (3, 2, 1, 0, 4):
        copies[level].start()

    def fill(part, carry):
        begin = pl.multiple_of(part * HALF, HALF)
        lanes = pl.ds(pl.multiple_of(part * 256, 256), 256)
        held = [tops[:, lanes].astype(F32), others[:, lanes].astype(F32)]
        gap = jnp.zeros((HALF - 2 * tops.shape[0], 256), F32)
        rows[pl.ds(begin, HALF), :] = jnp.concatenate(held + [gap], axis=0)
        return carry

    lax.fori_loop(0, 2, fill, 0)
    dense = jnp.transpose(rows[...])[:SIZE].astype(BF16)
    own_row = lax.axis_index("row")
    place = top_list[...] ^ own_row
    place = place ^ ((place >> 1) & 0b01010)
    mine = iota(place.shape, 1) == own_row
    listed = jnp.sum(jnp.where(mine, place.astype(F32), 0.0), axis=1, keepdims=True)
    codes = (iota((128, 128), 0) - (iota((128, 128), 1) & HALF)).astype(F32)
    select = jnp.concatenate([(codes == listed[k : k + 1, :]).astype(BF16) for k in range(ENTRIES)], axis=1)
    picked = mm(dense, select).astype(BF16)
    local = apply_each(transfer, lambda k: tile(picked, k), ENTRIES).astype(BF16)
    copies[3].wait()
    local = combine(mm(own_op[0], local), mm(own_op[1], local)).astype(BF16)
    lane = iota((SIZE, 128), 1) & 63
    for level, at_level, octant in ((2, low_near, lane >> 3), (1, mid_near, lane & 7)):
        copies[level].wait()
        by_real = mm(down[level, 0, 0], local)
        by_imag = mm(down[level, 0, 1], local)
        for c in range(1, OCTANTS):
            by_real = jnp.where(octant == c, mm(down[level, c, 0], local), by_real)
            by_imag = jnp.where(octant == c, mm(down[level, c, 1], local), by_imag)
        local = (combine(by_real, by_imag) + at_level[...]).astype(BF16)
    copies[0].wait()
    real, imag = [], []
    for pair in range(OCTANTS // 2):
        terms = [
            combine(mm(down[0, c, 0], local), mm(down[0, c, 1], local))
            for c in (2 * pair, 2 * pair + 1)
        ]
        one_real, one_imag = regroup(*terms)
        real.append(one_real)
        imag.append(one_imag)
    copies[4].wait()
    row = iota((FINE, FINE), 0)
    col = iota((FINE, FINE), 1)
    places = (row == (col & 7) * HALF + (col >> 3)).astype(BF16)
    out_copies = []
    for part, terms in enumerate((real, imag)):
        term = jnp.concatenate(terms, axis=1)
        high = term.astype(BF16)
        low = (term - high.astype(F32)).astype(BF16)
        for half in range(2):
            columns = pl.ds(half * REACH, REACH)
            place = places[:, half * REACH : (half + 1) * REACH]
            near = fine_b if half else fine_a
            out[part, :, columns] = near[part] + mm(high, place) + mm(low, place)
            copy = pltpu.make_async_copy(
                out.at[part, :, columns], out_hbm.at[part, :, columns], sems.at[6 + 2 * part + half]
            )
            copy.start()
            out_copies.append(copy)
    for copy in out_copies:
        copy.wait()


def shape(dims, dtype):
    return jax.ShapeDtypeStruct(dims, dtype)


VMEM = pl.BlockSpec(memory_space=pltpu.VMEM)
SMEM = pl.BlockSpec(memory_space=pltpu.SMEM)
HBM = pl.BlockSpec(memory_space=pltpu.HBM)
INTERPRET = False


def in_hbm(x):
    return x if INTERPRET else pltpu.with_memory_space_constraint(x, pltpu.HBM)


def on_chip(dims, dtype):
    return shape(dims, dtype) if INTERPRET else pltpu.VMEM(dims, dtype)


def off_chip(dims, dtype):
    return shape(dims, dtype) if INTERPRET else pltpu.HBM(dims, dtype)


def call(kernel, ins, outs, scratch, flops, limit=16, place=VMEM):
    return pl.pallas_call(
        kernel,
        in_specs=ins,
        out_specs=[place] * len(outs),
        out_shape=outs,
        scratch_shapes=scratch,
        compiler_params=pltpu.CompilerParams(vmem_limit_bytes=limit << 20),
        cost_estimate=pl.CostEstimate(flops=flops, bytes_accessed=8 << 20, transcendentals=0),
        interpret=INTERPRET,
    )


def body(
    check_field, to_equiv, upward_ops, downward_ops, transfer_ops, list_fine, list_mid, list_low, list_top
):
    axes = ("row", "col")
    rows, cols = lax.axis_size("row"), lax.axis_size("col")
    count = rows * cols
    check_field, to_equiv, upward_ops, downward_ops, transfer_ops = [
        in_hbm(x) for x in (check_field, to_equiv, upward_ops, downward_ops, transfer_ops)
    ]
    octant_ops = (2, SIZE, SIZE)
    to_left, to_right, own_small, top = call(
        up_kernel,
        [HBM, HBM, HBM],
        [
            shape((2 * SIZE + 80, REACH), BF16),
            shape((2 * SIZE + 80, REACH), BF16),
            shape((2 * SIZE, 128), BF16),
            shape((1, 512), F32),
        ],
        [
            pltpu.VMEM((2, SIZE, FINE), BF16),
            pltpu.VMEM(octant_ops, BF16),
            pltpu.VMEM((3, OCTANTS) + octant_ops, BF16),
            pltpu.VMEM(octant_ops, BF16),
            pltpu.VMEM((FINE, FINE), BF16),
            pltpu.SemaphoreType.DMA((6,)),
        ],
        4 << 30,
    )(check_field, to_equiv, upward_ops)
    from_left = lax.ppermute(to_right, axes, [(i, (i + 1) % count) for i in range(count)])
    from_right = lax.ppermute(to_left, axes, [(i, (i - 1) % count) for i in range(count)])

    def load(ride):
        return call(
            load_kernel,
            [VMEM, HBM],
            [shape(ride.shape, ride.dtype), on_chip((ENTRIES,) + octant_ops, BF16)],
            [pltpu.SemaphoreType.DMA(())],
            8 << 30,
        )(ride, transfer_ops)

    def small(kernel, listed, ride):
        return call(
            kernel,
            [VMEM] * 5 + [HBM],
            [shape(ride.shape, ride.dtype), shape((SIZE, 128), F32)],
            [pltpu.VMEM((ENTRIES,) + octant_ops, BF16), pltpu.SemaphoreType.DMA((2,))],
            3 << 30,
        )(ride, from_left, from_right, own_small, listed, transfer_ops)

    def fine(half, begin, size, earlier, ride):
        around = (from_left, to_left, to_right) if half == 0 else (to_left, to_right, from_right)
        place = off_chip if half == 0 else on_chip if earlier else shape
        return call(
            functools.partial(fine_kernel, (half, begin, size)),
            [VMEM] * 5 + [HBM] + [VMEM] * len(earlier),
            [shape(ride.shape, ride.dtype), place((2, SIZE, REACH), F32)],
            [
                pltpu.VMEM((2 * SIZE, 3 * REACH), BF16),
                pltpu.VMEM((size, SIZE, FINE), BF16),
                pltpu.VMEM((size,) + octant_ops, BF16),
                pltpu.SemaphoreType.DMA(()),
            ],
            size << 29,
        )(ride, *around, list_fine.T, transfer_ops, *earlier)

    def swap(x, axis, mask):
        return lax.ppermute(x, axis, [(i, i ^ mask) for i in range(lax.axis_size(axis))])

    work = {
        1: {"top": load},
        2: {"a": lambda ride: fine(0, 0, ENTRIES, [], ride)},
        4: {"mid": functools.partial(small, mid_kernel, list_mid.T)},
        5: {"low": functools.partial(small, low_kernel, list_low)},
        6: {"b": lambda ride: fine(1, 0, GROUP, [], ride)},
        7: {"b": lambda ride: fine(1, GROUP, ENTRIES - GROUP, done["b"], ride)},
    }
    done = {}
    total = top
    for step, mask in enumerate((1, 2, 6, 1, 2, 6, 8, 24)):
        axis = "col" if step < 3 else "row"
        other = swap(total, axis, mask) if axis == "col" or mask < rows else None
        for name, kernel in work.get(step, {}).items():
            total, *done[name] = kernel(total)
        if axis == "col":
            total = total + other
        elif step < 7:
            total = total if other is None else jnp.concatenate([total, other], axis=0)
        if step == 2:
            total = total.astype(BF16)
    other = total if other is None else other
    (far,) = call(
        down_kernel,
        [VMEM] * 3 + [HBM] + [VMEM] * 4 + [HBM],
        [shape((2, SIZE, FINE), F32)],
        [
            pltpu.VMEM((2, SIZE, FINE), F32),
            pltpu.VMEM((2, SIZE, REACH), F32),
            pltpu.VMEM((3, OCTANTS) + octant_ops, BF16),
            pltpu.VMEM(octant_ops, BF16),
            pltpu.VMEM((128, 256), F32),
            pltpu.SemaphoreType.DMA((10,)),
        ],
        8 << 30,
        place=HBM,
    )(
        total, other, list_top.T, in_hbm(done["a"][0]), *done["b"], *done["mid"], *done["low"],
        *done["top"],
        downward_ops,
    )
    return far


def solution(mesh):
    split = P(None, None, ("row", "col"))
    lists = P(("row", "col"), None)
    return jax.shard_map(
        body,
        mesh=mesh,
        in_specs=(split, P(), P(), P(), P(), lists, lists, lists, P()),
        out_specs=split,
        check_vma=False,
    )
```
